256 devices in a mesh: seq: 64 (over z, y, core), head: 4 (over x).
Axes of the slice: x: 4, y: 4, z: 8, core: 2. Of those that a mesh axis runs over, the one named last changes fastest.
Arguments:
- query_rows: bfloat16 [16384, 8192], P('seq', 'head'), may hold values from -1.796875 to 1.796875
- key_rows: bfloat16 [16384, 8192], P('seq', 'head'), may hold values from -1.796875 to 1.796875
- value_rows: bfloat16 [16384, 8192], P('seq', 'head'), may hold values from -20 to 20, as said below
- gate: bfloat16 [16384, 8192], P('seq', 'head'), may hold values from -6 to 6
- log_decay: float32 [16384, 64], P('seq', 'head'), may hold values from -1 to 0, as said below
- gain: float32 [8192], P('head'), may hold values from 0.1 to 1.9
- grad_mixed: bfloat16 [16384, 8192], P('seq', 'head'), may hold values from -6 to 6
Outputs:
- mixed: bfloat16 [16384, 8192], P('seq', 'head')
- grad_query: bfloat16 [16384, 8192], P('seq', 'head')
- grad_key: bfloat16 [16384, 8192], P('seq', 'head')
- grad_value: bfloat16 [16384, 8192], P('seq', 'head')
- grad_gate: bfloat16 [16384, 8192], P('seq', 'head')
The draws below stay inside these ranges and needn't reach their ends.
Inputs may be any that keep to these rules, and one draw needn't show every extreme that they name: `value_rows`: values of the heads differ in scale. `log_decay`: Per-token log decays; rates differ over heads and tokens.
All inputs are finite; a program needn't handle non-finite values.
Results may differ from the reference program's by a relative error of at most 0.006.
Values sent between devices are 32-bit elements; how exact they have to be, the bound alone decides.
No kernel may reach another device: no remote copies, remote signals or barrier semaphores. Data moves between devices by JAX's collectives and lax.ppermute only.
A program may use at most 192 MiB of HBM per device.

```python
import jax
import jax.numpy as jnp
from jax import lax

HEAD_COUNT = 64
DH = 128
GROUP = 256
TOK_DEV = 256
TOKEN_COUNT = 16384


def draw_value_rows(key, part):
    key = jax.random.fold_in(key, 11)
    first, second = jax.random.split(key)
    base = jax.random.normal(first, (TOKEN_COUNT, HEAD_COUNT * DH), jnp.float32)
    spread = 3.0
    base = jnp.clip(base, -4.0, 4.0)
    position = jnp.arange(HEAD_COUNT, dtype=jnp.float32) / max(HEAD_COUNT - 1, 1)
    factor = jax.random.uniform(second, (HEAD_COUNT,), jnp.float32, 0.8, 1.25)
    scale = jnp.repeat(spread ** position * factor, DH)
    return (base * scale[None, :]).astype(jnp.bfloat16)


def draw_log_decay(key, part):
    key = jax.random.fold_in(key, 23)
    key_collection = jax.random.split(key, 7)
    fast_share = 0.5
    fast = jax.random.uniform(key_collection[0], (HEAD_COUNT,), jnp.float32) < fast_share
    fast_rate = jnp.exp(jax.random.uniform(key_collection[1], (HEAD_COUNT,), jnp.float32, jnp.log(1.0 / 50.0), jnp.log(1.0 / 30.0)))
    slow_rate = jnp.exp(jax.random.uniform(key_collection[2], (HEAD_COUNT,), jnp.float32, jnp.log(0.05), jnp.log(0.3))) / TOKEN_COUNT
    decay_speed = jnp.where(fast, fast_rate, slow_rate)
    block_multiple = jnp.exp(jax.random.uniform(key_collection[3], (TOKEN_COUNT // TOK_DEV, HEAD_COUNT), jnp.float32, jnp.log(0.5), jnp.log(2.0)))
    block_multiple = jnp.repeat(block_multiple, TOK_DEV, axis=0)
    random_noise = jax.random.uniform(key_collection[4], (TOKEN_COUNT, HEAD_COUNT), jnp.float32, 0.5, 1.5)
    spike_amount = jax.random.uniform(key_collection[5], (TOKEN_COUNT, HEAD_COUNT), jnp.float32) < 2.0 / TOKEN_COUNT
    training_objective = jax.random.uniform(key_collection[6], (TOKEN_COUNT, HEAD_COUNT), jnp.float32, 0.2, 0.5)
    return -decay_speed[None, :] * block_multiple * random_noise + jnp.where(spike_amount, jnp.log(1.0 - training_objective), 0.0)


def steps_of(stream_key, shape, cuts, least, top_value):
    def one(axis_at, blocks):
        heights = jax.random.uniform(jax.random.fold_in(jax.random.fold_in(stream_key, 6), axis_at), (blocks,), jnp.float32, least / len(cuts), top_value / len(cuts))
        return jnp.repeat(jnp.exp(heights), shape[axis_at] // blocks).reshape((-1,) + (1,) * (len(shape) - axis_at - 1))

    factor_of = one(*cuts[0])
    for cut in cuts[1:]:
        factor_of = factor_of * one(*cut)
    return factor_of


def noise(rng, extent, scale, reach, pieces=(), kind=jnp.bfloat16):
    values = scale * jax.random.normal(rng, extent, jnp.float32)
    if pieces:
        values = values * steps_of(rng, extent, pieces, -0.22, 0.18)
    return jnp.clip(values, -reach, reach).astype(kind)


def setup_inputs(seed: int = 0) -> dict:
    splits = jax.random.split(jax.random.key(seed), 8)
    return {
        "query_rows": noise(splits[0], (TOKEN_COUNT, HEAD_COUNT * DH), 0.3, 1.796875, ((0, 64), (1, 4))),
        "key_rows": noise(splits[1], (TOKEN_COUNT, HEAD_COUNT * DH), 0.3, 1.796875, ((0, 64), (1, 4))),
        "value_rows": draw_value_rows(jax.random.fold_in(splits[7], 71), 0),
        "gate": noise(splits[3], (TOKEN_COUNT, HEAD_COUNT * DH), 1.0, 6.0, ((0, 64), (1, 4))),
        "log_decay": draw_log_decay(jax.random.fold_in(splits[7], 71), 0),
        "gain": jnp.clip(1.0 + 0.18 * jax.random.normal(splits[5], (HEAD_COUNT * DH,), jnp.float32), 0.1, 1.9),
        "grad_mixed": noise(splits[6], (TOKEN_COUNT, HEAD_COUNT * DH), 1.0, 6.0, ((0, 64), (1, 4))),
    }


EPSILON = 1e-06

def rounded(values):
    return lax.optimization_barrier(values.astype(jnp.bfloat16)).astype(jnp.float32)

def decay_table(decays):
    cumulative = jnp.cumsum(decays, axis=0)
    across = cumulative.T
    length = across.shape[1]
    rows = lax.broadcasted_iota(jnp.int32, (length, length), 0)
    columns = lax.broadcasted_iota(jnp.int32, (length, length), 1)
    gaps = across[:, :, None] - across[:, None, :]
    weights = jnp.exp(jnp.where((rows >= columns)[None], gaps, -jnp.inf))
    return (cumulative, weights)

def forward_group(state, inputs):
    query, keys, value, decays = inputs
    cumulative, weights = decay_table(decays)
    scores = jnp.einsum('thd,shd->hts', query, keys)
    probs = rounded(scores * weights)
    intra = jnp.einsum('hts,shd->thd', probs, value)
    inter = jnp.einsum('thd,hde->the', query, rounded(state)) * jnp.exp(cumulative)[:, :, None]
    last = cumulative[-1]
    keyed = rounded(keys * jnp.exp(last[None, :] - cumulative)[:, :, None])
    local = jnp.einsum('thd,the->hde', keyed, value)
    return (jnp.exp(last)[:, None, None] * state + local, (intra + inter, state))

def backward_group(after, inputs):
    query, keys, value, decays, grad_out, before = inputs
    cumulative, weights = decay_table(decays)
    last = cumulative[-1]
    probs = rounded(jnp.einsum('thd,shd->hts', query, keys) * weights)
    grad_scores = rounded(jnp.einsum('thd,shd->hts', grad_out, value) * weights)
    toward_start = jnp.exp(cumulative)[:, :, None]
    toward_end = jnp.exp(last[None, :] - cumulative)[:, :, None]
    after_low = rounded(after)
    grad_q = jnp.einsum('hts,shd->thd', grad_scores, keys)
    grad_q = grad_q + jnp.einsum('the,hde->thd', grad_out, rounded(before)) * toward_start
    grad_k = jnp.einsum('hts,thd->shd', grad_scores, query)
    grad_k = grad_k + jnp.einsum('she,hde->shd', value, after_low) * toward_end
    grad_v = jnp.einsum('hts,the->she', probs, grad_out)
    grad_v = grad_v + jnp.einsum('shd,hde->she', keys, after_low) * toward_end
    weighted = rounded(query * toward_start)
    term = jnp.einsum('thd,the->hde', weighted, grad_out)
    updated = jnp.exp(last)[:, None, None] * after + term
    return (updated, (grad_q.astype(jnp.bfloat16), grad_k.astype(jnp.bfloat16), grad_v.astype(jnp.bfloat16)))

def reference(query_rows, key_rows, value_rows, gate, log_decay, gain, grad_mixed):
    blocks = TOKEN_COUNT // GROUP

    def split(values):
        return values.astype(jnp.float32).reshape(blocks, GROUP, HEAD_COUNT, DH)
    query = split(query_rows)
    keys = split(key_rows)
    value = split(value_rows)
    decays = log_decay.astype(jnp.float32).reshape(blocks, GROUP, HEAD_COUNT)
    zero_state = jnp.zeros((HEAD_COUNT, DH, DH), jnp.float32)
    unused, (attention, befores) = lax.scan(forward_group, zero_state, (query, keys, value, decays))
    attention = attention.reshape(TOKEN_COUNT, HEAD_COUNT * DH)
    scale = lax.rsqrt(lax.optimization_barrier(jnp.mean(attention * attention, axis=1, keepdims=True)) + EPSILON)
    normed = attention * scale
    shaped = normed * gain
    opening = jax.nn.sigmoid(gate.astype(jnp.float32))
    mixed = (shaped * opening).astype(jnp.bfloat16)
    upstream = grad_mixed.astype(jnp.float32)
    grad_gate = (upstream * shaped * opening * (1.0 - opening)).astype(jnp.bfloat16)
    grad_normed = upstream * opening * gain
    projection = lax.optimization_barrier(jnp.mean(grad_normed * normed, axis=1, keepdims=True))
    grad_attention = rounded(scale * (grad_normed - normed * projection))
    grad_attention = grad_attention.reshape(blocks, GROUP, HEAD_COUNT, DH)
    unused_after, (grad_q, grad_k, grad_v) = lax.scan(backward_group, zero_state, (query, keys, value, decays, grad_attention, befores), reverse=True)
    grad_q = grad_q.reshape(TOKEN_COUNT, HEAD_COUNT * DH)
    grad_k = grad_k.reshape(TOKEN_COUNT, HEAD_COUNT * DH)
    grad_v = grad_v.reshape(TOKEN_COUNT, HEAD_COUNT * DH)
    return (mixed, grad_q, grad_k, grad_v, grad_gate)
```

```python
import functools

import jax
import jax.numpy as jnp
from jax import lax
from jax.experimental import pallas as pl
from jax.experimental.pallas import tpu as pltpu
from jax.sharding import Mesh, PartitionSpec as P

DH = 128
GROUP = 256
HALF = 8
WIDE = HALF * DH
FEATURES = 64 * DH
EPSILON = 1e-06
F32 = jnp.float32
BF16 = jnp.bfloat16
PLANE = ("z0", "y")
VMEM = pl.BlockSpec(memory_space=pltpu.VMEM)
SMEM = pl.BlockSpec(memory_space=pltpu.SMEM)


def call(kernel, out, *args, flops=0, smem=1, limit=12, name=None):
    moved = sum(a.size * a.dtype.itemsize for a in args)
    moved += sum(o.size * o.dtype.itemsize for o in jax.tree.leaves(out))
    return pl.pallas_call(
        kernel,
        out_shape=out,
        in_specs=[SMEM] * smem + [VMEM] * (len(args) - smem),
        out_specs=jax.tree.map(lambda _: VMEM, out),
        compiler_params=pltpu.CompilerParams(vmem_limit_bytes=limit << 20),
        cost_estimate=pl.CostEstimate(flops=flops, bytes_accessed=moved, transcendentals=0),
        name=name,
    )(*args)


def shape(*dims, dtype=F32):
    return jax.ShapeDtypeStruct(dims, dtype)


def dot(a, b, ca, cb, precision=None):
    return lax.dot_general(
        a, b, (((ca,), (cb,)), ((), ())), precision=precision, preferred_element_type=F32
    )


def columns(role, core, i):
    side = core if role == 0 else 1 - core
    return pl.ds(pl.multiple_of(side * WIDE + i * DH, DH), DH)


def lanes(tab, which, role, i):
    at = which * 16 + role * HALF + i
    return tab[:, at : at + 1]


def tables(core, decays):
    rows = lax.broadcasted_iota(jnp.int32, (GROUP, GROUP), 0)
    cols = lax.broadcasted_iota(jnp.int32, (GROUP, GROUP), 1)
    tri = (rows >= cols).astype(F32)
    down = dot(tri, decays, 1, 0, lax.Precision.HIGHEST)
    across = dot(decays, tri, 0, 1, lax.Precision.HIGHEST)
    swapped = jnp.concatenate([down[:, HALF:], down[:, :HALF]], axis=1)
    down = jnp.where(core == 0, down, swapped)
    across = jnp.where(core == 0, across, jnp.concatenate([across[HALF:], across[:HALF]], axis=0))
    return down, across


def state_term(core, role, i, keys_ref, value_ref, tab):
    at = columns(role, core, i)
    keyed = (keys_ref[:, at].astype(F32) * lanes(tab, 2, role, i)).astype(BF16)
    return dot(keyed, value_ref[:, at], 0, 0)


def first_kernel(core_ref, keys_ref, value_ref, decay_ref, tab_ref, across_ref, send_ref):
    core = core_ref[0]
    down, across = tables(core, decay_ref[...])
    last = down[GROUP - 1 :, :]
    blank = jnp.zeros((GROUP, 128 - 48), F32)
    tab = jnp.concatenate([down, jnp.exp(down), jnp.exp(last - down), blank], axis=1)
    tab_ref[...] = tab
    across_ref[...] = across
    for i in range(HALF):
        send_ref[i * DH : (i + 1) * DH, :] = state_term(core, 1, i, keys_ref, value_ref, tab)
    send_ref[WIDE:, :] = jnp.broadcast_to(tab[GROUP - 1 :, :], (8, 128))


def second_kernel(core_ref, keys_ref, value_ref, tab_ref, keep_ref):
    core = core_ref[0]
    tab = tab_ref[...]
    for i in range(HALF):
        keep_ref[i * DH : (i + 1) * DH, :] = state_term(core, 0, i, keys_ref, value_ref, tab)


def merge_forward(core_ref, own_ref, other_ref, tab_ref, out_ref, dec_ref):
    zero = core_ref[0] == 0
    mine = tab_ref[GROUP - 1 :, :HALF]
    theirs = other_ref[WIDE : WIDE + 1, HALF : 2 * HALF]
    last_a = jnp.where(zero, mine, theirs)
    last_b = jnp.where(zero, theirs, mine)
    for i in range(HALF):
        own = own_ref[i * DH : (i + 1) * DH, :]
        other = other_ref[i * DH : (i + 1) * DH, :]
        a, b = jnp.where(zero, own, other), jnp.where(zero, other, own)
        here_a = jnp.broadcast_to(last_a[:, i : i + 1], (1, 128))
        here_b = jnp.broadcast_to(last_b[:, i : i + 1], (1, 128))
        dec_ref[i : i + 1, :] = jnp.exp(here_a)
        dec_ref[HALF + i : HALF + i + 1, :] = jnp.exp(here_b)
        out_ref[i, :DH, :] = jnp.exp(here_b) * a + b
        out_ref[i, DH:, :] = jnp.broadcast_to(here_a + here_b, (8, 128))


def merge_backward(core_ref, own_ref, other_ref, dec_ref, out_ref):
    zero = core_ref[0] == 0
    for i in range(HALF):
        own = own_ref[i * DH : (i + 1) * DH, :]
        other = other_ref[i * DH : (i + 1) * DH, :]
        a, b = jnp.where(zero, own, other), jnp.where(zero, other, own)
        out_ref[i] = a + dec_ref[i : i + 1, :] * b


def total_kernel(reverse, parts_ref, decays_ref, out_ref):
    order = list(range(8))[:: -1 if reverse else 1]
    total = parts_ref[order[0], :DH, :]
    for at in order[1:]:
        total = jnp.exp(decays_ref[at, DH : DH + 1, :]) * total + parts_ref[at, :DH, :]
    out_ref[:DH, :] = total
    decay = decays_ref[0, DH:, :]
    for at in range(1, 8):
        decay = decay + decays_ref[at, DH:, :]
    out_ref[DH:, :] = decay


def enter_kernel(reverse, parts_ref, decays_ref, near_ref, mid_ref, far_ref, out_ref):
    state = far_ref[:DH, :]
    for ref in (mid_ref, near_ref):
        state = jnp.exp(ref[DH : DH + 1, :]) * state + ref[:DH, :]
    order = list(range(8))[:: -1 if reverse else 1]
    for at in order:
        out_ref[at] = state
        if at != order[-1]:
            state = jnp.exp(decays_ref[at, DH : DH + 1, :]) * state + parts_ref[at, :DH, :]


def leave_kernel(reverse, core_ref, enter_ref, own_ref, other_ref, dec_ref, keep_ref, send_ref):
    first = core_ref[0] == (1 if reverse else 0)
    base = HALF if reverse else 0
    for i in range(HALF):
        own = own_ref[i * DH : (i + 1) * DH, :]
        other = other_ref[i * DH : (i + 1) * DH, :]
        nearer = jnp.where(first, own, other)
        x = enter_ref[i]
        y = dec_ref[base + i : base + i + 1, :] * x + nearer
        keep_ref[i] = jnp.where(first, x, y)
        send_ref[i] = jnp.where(first, y, x)


def weights_of(tab, across_ref, role, i):
    rows = lax.broadcasted_iota(jnp.int32, (GROUP, GROUP), 0)
    cols = lax.broadcasted_iota(jnp.int32, (GROUP, GROUP), 1)
    at = role * HALF + i
    gaps = lanes(tab, 0, role, i) - across_ref[at : at + 1, :]
    return jnp.exp(jnp.where(rows >= cols, gaps, -jnp.inf))


def intra_kernel(
    role, core_ref, query_ref, keys_ref, value_ref, gate_ref, gain_ref, mixed_ref, tab_ref, across_ref,
    intra_ref, normed_ref,
):
    core = core_ref[0]
    tab = tab_ref[...]
    for i in range(HALF):
        at = columns(role, core, i)
        to = slice(i * DH, (i + 1) * DH)
        scores = dot(query_ref[:, at], keys_ref[:, at], 1, 1)
        probs = (scores * weights_of(tab, across_ref, role, i)).astype(BF16)
        intra_ref[:, to] = dot(probs, value_ref[:, at], 1, 0)
        opening = jax.nn.sigmoid(gate_ref[:, at].astype(F32))
        normed_ref[:, to] = mixed_ref[:, at].astype(F32) * opening * gain_ref[:, at]


def attend_kernel(role, core_ref, query_ref, state_ref, intra_ref, normed_ref, tab_ref, sums_ref, out_ref, add_ref):
    core = core_ref[0]
    tab = tab_ref[...]
    squares = jnp.zeros((GROUP, DH), F32)
    products = jnp.zeros((GROUP, DH), F32)
    for i in range(HALF):
        at = columns(role, core, i)
        to = slice(i * DH, (i + 1) * DH)
        inter = dot(query_ref[:, at], state_ref[i].astype(BF16), 1, 0)
        attention = intra_ref[:, to] + inter * lanes(tab, 1, role, i)
        out_ref[:, to] = attention
        squares = squares + attention * attention
        products = products + normed_ref[:, to] * attention
    ones = jnp.ones((8, DH), F32)
    squares = dot(ones, squares, 1, 1, lax.Precision.HIGHEST)
    products = dot(ones, products, 1, 1, lax.Precision.HIGHEST)
    row = lax.broadcasted_iota(jnp.int32, (8, GROUP), 0)
    both = jnp.where(row == 0, squares, products)
    add_ref[...] = both if sums_ref is None else sums_ref[...] + both


def upright(row):
    rows = lax.broadcasted_iota(jnp.int32, (GROUP, GROUP), 0)
    cols = lax.broadcasted_iota(jnp.int32, (GROUP, GROUP), 1)
    return jnp.sum(jnp.where(rows == cols, row, 0.0), axis=1, keepdims=True)


def norm_terms(sums_ref):
    scale = lax.rsqrt(sums_ref[0:1, :] / FEATURES + EPSILON)
    projection = scale * sums_ref[1:2, :] / FEATURES
    return upright(scale), upright(projection)


def grad_kernel(role, core_ref, query_ref, attention_ref, normed_ref, tab_ref, sums_ref, grad_ref, term_ref):
    core = core_ref[0]
    tab = tab_ref[...]
    scale, projection = norm_terms(sums_ref)
    for i in range(HALF):
        at = columns(role, core, i)
        to = slice(i * DH, (i + 1) * DH)
        normed = attention_ref[:, to] * scale
        grad = (scale * (normed_ref[:, to] - normed * projection)).astype(BF16)
        grad_ref[:, to] = grad
        weighted = (query_ref[:, at].astype(F32) * lanes(tab, 1, role, i)).astype(BF16)
        term_ref[i * DH : (i + 1) * DH, :] = dot(weighted, grad, 0, 0)


def inner_kernel(
    role, core_ref, query_ref, keys_ref, value_ref, state_ref, grad_ref, tab_ref, across_ref,
    query_out, keys_out, value_out,
):
    core = core_ref[0]
    tab = tab_ref[...]
    for i in range(HALF):
        at = columns(role, core, i)
        to = slice(i * DH, (i + 1) * DH)
        query, keys, value, grad = query_ref[:, at], keys_ref[:, at], value_ref[:, at], grad_ref[:, to]
        weights = weights_of(tab, across_ref, role, i)
        probs = (dot(query, keys, 1, 1) * weights).astype(BF16)
        grad_scores = (dot(grad, value, 1, 1) * weights).astype(BF16)
        grad_query = dot(grad_scores, keys, 1, 0)
        grad_query = grad_query + dot(grad, state_ref[i].astype(BF16), 1, 1) * lanes(tab, 1, role, i)
        query_out[:, to] = grad_query.astype(BF16)
        keys_out[:, to] = dot(grad_scores, query, 0, 0)
        value_out[:, to] = dot(probs, grad, 0, 0)


def gate_kernel(
    core_ref, gate_ref, gain_ref, upstream_ref, own_ref, other_ref, own_query, other_query, sums_ref,
    mixed_out, gate_out, query_out,
):
    core = core_ref[0]
    scale, _ = norm_terms(sums_ref)
    for role, ref, grad_query in ((0, own_ref, own_query), (1, other_ref, other_query)):
        for i in range(HALF):
            at = columns(role, core, i)
            to = slice(i * DH, (i + 1) * DH)
            shaped = ref[:, to] * scale * gain_ref[:, at]
            opening = jax.nn.sigmoid(gate_ref[:, at].astype(F32))
            mixed_out[:, at] = (shaped * opening).astype(BF16)
            upstream = upstream_ref[:, at].astype(F32)
            gate_out[:, at] = (upstream * shaped * opening * (1.0 - opening)).astype(BF16)
            query_out[:, at] = grad_query[:, to]


def last_kernel(
    core_ref, keys_ref, value_ref, own_state, other_state, own_keys, other_keys, own_value, other_value, tab_ref,
    keys_out, value_out,
):
    core = core_ref[0]
    tab = tab_ref[...]
    parts = ((0, own_state, own_keys, own_value), (1, other_state, other_keys, other_value))
    for role, state_ref, part_keys, part_value in parts:
        for i in range(HALF):
            at = columns(role, core, i)
            to = slice(i * DH, (i + 1) * DH)
            state = state_ref[i].astype(BF16)
            toward_end = lanes(tab, 2, role, i)
            grad_keys = part_keys[:, to] + dot(value_ref[:, at], state, 1, 1) * toward_end
            grad_value = part_value[:, to] + dot(keys_ref[:, at], state, 1, 0) * toward_end
            keys_out[:, at] = grad_keys.astype(BF16)
            value_out[:, at] = grad_value.astype(BF16)


def swap(array):
    return lax.ppermute(array, "core", [(0, 1), (1, 0)])


def shifted(array, by):
    return lax.ppermute(array, "z1", [(i, i + by) for i in range(4) if 0 <= i + by < 4])


def spread(array):
    return lax.all_to_all(array, PLANE, 0, 0, tiled=True)


def across_heads(array):
    for flip in (1, 3):
        array = array + lax.ppermute(array, "head", [(i, i ^ flip) for i in range(4)])
    return array


def scan(core, own, other, tab, dec, decays, reverse):
    if reverse:
        totals = call(merge_backward, shape(HALF, DH, DH), core, own, other, dec, name="merge_b")
    else:
        totals, dec = call(
            merge_forward, (shape(HALF, DH + 8, DH), shape(2 * HALF, DH)), core, own, other, tab, name="merge_f"
        )
    parts = spread(totals)
    decays = parts if decays is None else decays
    row = call(
        functools.partial(total_kernel, reverse), shape(DH + 8, DH), parts, decays, smem=0, name="row_total"
    )
    step = -1 if reverse else 1
    near, mid, far = (shifted(row, step * by) for by in (1, 2, 3))
    entering = call(
        functools.partial(enter_kernel, reverse), shape(8, DH, DH), parts, decays, near, mid, far, smem=0, name="enter"
    )
    entering = spread(entering)
    keep, send = call(
        functools.partial(leave_kernel, reverse),
        (shape(HALF, DH, DH), shape(HALF, DH, DH)),
        core, entering, own, other, dec, name="leave",
    )
    return keep, swap(send), dec, decays


def on_device(query, keys, value, gate, decay, gain, upstream):
    core = lax.axis_index("core").astype(jnp.int32).reshape(1)
    gain = gain.reshape(1, -1)
    big = 2 * GROUP * GROUP * DH * HALF
    small = big // 2

    tab, across, send = call(
        first_kernel,
        (shape(GROUP, 128), shape(16, GROUP), shape(WIDE + 8, DH)),
        core, keys, value, decay, flops=small, name="first",
    )
    other = swap(send)
    own = call(second_kernel, shape(WIDE, DH), core, keys, value, tab, flops=small, name="second")

    wide = shape(GROUP, WIDE)
    intra = [
        call(
            functools.partial(intra_kernel, role), (wide, wide),
            core, query, keys, value, gate, gain, upstream, tab, across, flops=2 * big, name=f"intra{role}",
        )
        for role in (0, 1)
    ]

    state_own, state_other, dec, decays = scan(core, own, other, tab, None, None, False)

    def attend_first(core_ref, query_ref, state_ref, intra_ref, normed_ref, tab_ref, out_ref, add_ref):
        attend_kernel(0, core_ref, query_ref, state_ref, intra_ref, normed_ref, tab_ref, None, out_ref, add_ref)

    sums_shape = shape(8, GROUP)
    att_own, sums = call(
        attend_first, (wide, sums_shape), core, query, state_own, *intra[0], tab, flops=small, name="attend0"
    )
    att_other, sums = call(
        functools.partial(attend_kernel, 1), (wide, sums_shape),
        core, query, state_other, *intra[1], tab, sums, flops=small, name="attend1",
    )
    sums = across_heads(sums)

    grads_shape = (shape(GROUP, WIDE, dtype=BF16), shape(WIDE, DH))
    grad_other, term_send = call(
        functools.partial(grad_kernel, 1), grads_shape, core, query, att_other, intra[1][1], tab, sums,
        flops=small, name="grad1",
    )
    term_other = swap(term_send)
    grad_own, term_own = call(
        functools.partial(grad_kernel, 0), grads_shape, core, query, att_own, intra[0][1], tab, sums,
        flops=small, name="grad0",
    )

    inner = [
        call(
            functools.partial(inner_kernel, role), (shape(GROUP, WIDE, dtype=BF16), wide, wide),
            core, query, keys, value, state, grad, tab, across, flops=6 * big, name=f"inner{role}",
        )
        for role, state, grad in ((0, state_own, grad_own), (1, state_other, grad_other))
    ]
    full = shape(GROUP, 2 * WIDE, dtype=BF16)
    mixed, grad_gate, grad_query = call(
        gate_kernel, (full, full, full),
        core, gate, gain, upstream, att_own, att_other, inner[0][0], inner[1][0], sums, name="gates", limit=20,
    )

    after_own, after_other, _, _ = scan(core, term_own, term_other, tab, dec, decays, True)
    grad_keys, grad_value = call(
        last_kernel, (full, full),
        core, keys, value, after_own, after_other, inner[0][1], inner[1][1], inner[0][2], inner[1][2], tab,
        flops=4 * small, name="last", limit=20,
    )
    return mixed, grad_query, grad_keys, grad_value, grad_gate


def solution(mesh):
    levels = Mesh(mesh.devices.reshape(4, 2, 4, 2, 4), ("z1", "z0", "y", "core", "head"))
    seq = ("z1", "z0", "y", "core")
    both = P(seq, "head")
    return jax.shard_map(
        on_device,
        mesh=levels,
        in_specs=(both, both, both, both, both, P("head"), both),
        out_specs=(both,) * 5,
        check_vma=False,
    )
```

```python
import functools

import jax
import jax.numpy as jnp
from jax import lax
from jax.experimental import pallas as pl
from jax.experimental.pallas import tpu as pltpu
from jax.sharding import Mesh, PartitionSpec as P

DH = 128
GROUP = 256
HALF = 8
WIDE = HALF * DH
FEATURES = 64 * DH
EPSILON = 1e-06
F32 = jnp.float32
BF16 = jnp.bfloat16
PLANE = ("z0", "y")
VMEM = pl.BlockSpec(memory_space=pltpu.VMEM)
SMEM = pl.BlockSpec(memory_space=pltpu.SMEM)
HBM = pl.BlockSpec(memory_space=pltpu.HBM)


def call(kernel, out, *args, flops=0, smem=1, limit=12, name=None, specs=None, outs=None, scratch=(), aliases=None):
    moved = sum(a.size * a.dtype.itemsize for a in args)
    moved += sum(o.size * o.dtype.itemsize for o in jax.tree.leaves(out))
    return pl.pallas_call(
        kernel,
        out_shape=out,
        in_specs=specs or [SMEM] * smem + [VMEM] * (len(args) - smem),
        out_specs=outs or jax.tree.map(lambda _: VMEM, out),
        scratch_shapes=scratch,
        input_output_aliases=aliases or {},
        compiler_params=pltpu.CompilerParams(vmem_limit_bytes=limit << 20),
        cost_estimate=pl.CostEstimate(flops=flops, bytes_accessed=moved, transcendentals=0),
        name=name,
    )(*args)


def shape(*dims, dtype=F32):
    return jax.ShapeDtypeStruct(dims, dtype)


def dot(a, b, ca, cb, precision=None):
    return lax.dot_general(
        a, b, (((ca,), (cb,)), ((), ())), precision=precision, preferred_element_type=F32
    )


def columns(role, core, i):
    side = core if role == 0 else 1 - core
    return pl.ds(pl.multiple_of(side * WIDE + i * DH, DH), DH)


def lanes(tab, which, role, i):
    at = which * 16 + role * HALF + i
    return tab[:, at : at + 1]


def tables(core, decays):
    rows = lax.broadcasted_iota(jnp.int32, (GROUP, GROUP), 0)
    cols = lax.broadcasted_iota(jnp.int32, (GROUP, GROUP), 1)
    tri = (rows >= cols).astype(F32)
    down = dot(tri, decays, 1, 1, lax.Precision.HIGHEST)
    across = dot(decays, tri, 1, 1, lax.Precision.HIGHEST)
    swapped = jnp.concatenate([down[:, HALF:], down[:, :HALF]], axis=1)
    down = jnp.where(core == 0, down, swapped)
    across = jnp.where(core == 0, across, jnp.concatenate([across[HALF:], across[:HALF]], axis=0))
    return down, across


def state_term(core, role, i, keys_ref, value_ref, tab):
    at = columns(role, core, i)
    keyed = (keys_ref[:, at].astype(F32) * lanes(tab, 2, role, i)).astype(BF16)
    return dot(keyed, value_ref[:, at], 0, 0)


def first_kernel(
    core_ref, keys_hbm, value_hbm, decay_hbm, tab_ref, across_ref, send_ref, keys_ref, value_ref, decay_ref, sems
):
    core = core_ref[0]
    copies = [pltpu.make_async_copy(decay_hbm, decay_ref, sems.at[0])]
    for role in (1, 0):
        at = pl.ds(pl.multiple_of((core if role == 0 else 1 - core) * WIDE, WIDE), WIDE)
        for source, target in ((keys_hbm, keys_ref), (value_hbm, value_ref)):
            copies.append(pltpu.make_async_copy(source.at[:, at], target.at[:, at], sems.at[len(copies)]))
    for copy in copies:
        copy.start()
    copies[0].wait()
    down, across = tables(core, decay_ref[...])
    last = down[GROUP - 1 :, :]
    blank = jnp.zeros((GROUP, 128 - 48), F32)
    tab = jnp.concatenate([down, jnp.exp(down), jnp.exp(last - down), blank], axis=1)
    tab_ref[...] = tab
    across_ref[...] = across
    send_ref[WIDE:, :] = jnp.broadcast_to(tab[GROUP - 1 :, :], (8, 128))
    copies[1].wait()
    copies[2].wait()
    for i in range(HALF):
        send_ref[i * DH : (i + 1) * DH, :] = state_term(core, 1, i, keys_ref, value_ref, tab)
    copies[3].wait()
    copies[4].wait()


def second_kernel(core_ref, keys_ref, value_ref, tab_ref, keep_ref):
    core = core_ref[0]
    tab = tab_ref[...]
    for i in range(HALF):
        keep_ref[i * DH : (i + 1) * DH, :] = state_term(core, 0, i, keys_ref, value_ref, tab)


def merge_forward(core_ref, own_ref, other_ref, tab_ref, out_ref, dec_ref):
    zero = core_ref[0] == 0
    mine = tab_ref[GROUP - 1 :, :HALF]
    theirs = other_ref[WIDE : WIDE + 1, HALF : 2 * HALF]
    last_a = jnp.where(zero, mine, theirs)
    last_b = jnp.where(zero, theirs, mine)
    for i in range(HALF):
        own = own_ref[i * DH : (i + 1) * DH, :]
        other = other_ref[i * DH : (i + 1) * DH, :]
        a, b = jnp.where(zero, own, other), jnp.where(zero, other, own)
        here_a = jnp.broadcast_to(last_a[:, i : i + 1], (1, 128))
        here_b = jnp.broadcast_to(last_b[:, i : i + 1], (1, 128))
        dec_ref[i : i + 1, :] = jnp.exp(here_a)
        dec_ref[HALF + i : HALF + i + 1, :] = jnp.exp(here_b)
        out_ref[i, :DH, :] = jnp.exp(here_b) * a + b
        out_ref[i, DH:, :] = jnp.broadcast_to(here_a + here_b, (8, 128))


def merge_backward(core_ref, own_ref, other_ref, dec_ref, out_ref):
    zero = core_ref[0] == 0
    for i in range(HALF):
        own = own_ref[i * DH : (i + 1) * DH, :]
        other = other_ref[i * DH : (i + 1) * DH, :]
        a, b = jnp.where(zero, own, other), jnp.where(zero, other, own)
        out_ref[i] = a + dec_ref[i : i + 1, :] * b


def total_kernel(reverse, parts_ref, decays_ref, out_ref):
    order = list(range(8))[:: -1 if reverse else 1]
    total = parts_ref[order[0], :DH, :]
    for at in order[1:]:
        total = jnp.exp(decays_ref[at, DH : DH + 1, :]) * total + parts_ref[at, :DH, :]
    out_ref[:DH, :] = total
    decay = decays_ref[0, DH:, :]
    for at in range(1, 8):
        decay = decay + decays_ref[at, DH:, :]
    out_ref[DH:, :] = decay


def enter_kernel(reverse, parts_ref, decays_ref, near_ref, mid_ref, far_ref, out_ref):
    state = far_ref[:DH, :]
    for ref in (mid_ref, near_ref):
        state = jnp.exp(ref[DH : DH + 1, :]) * state + ref[:DH, :]
    order = list(range(8))[:: -1 if reverse else 1]
    for at in order:
        out_ref[at] = state
        if at != order[-1]:
            state = jnp.exp(decays_ref[at, DH : DH + 1, :]) * state + parts_ref[at, :DH, :]


def leave_kernel(reverse, core_ref, enter_ref, own_ref, other_ref, dec_ref, keep_ref, send_ref):
    first = core_ref[0] == (1 if reverse else 0)
    base = HALF if reverse else 0
    for i in range(HALF):
        own = own_ref[i * DH : (i + 1) * DH, :]
        other = other_ref[i * DH : (i + 1) * DH, :]
        nearer = jnp.where(first, own, other)
        x = enter_ref[i]
        y = dec_ref[base + i : base + i + 1, :] * x + nearer
        keep_ref[i] = jnp.where(first, x, y)
        send_ref[i] = jnp.where(first, y, x)


def weights_of(tab, across_ref, role, i):
    rows = lax.broadcasted_iota(jnp.int32, (GROUP, GROUP), 0)
    cols = lax.broadcasted_iota(jnp.int32, (GROUP, GROUP), 1)
    at = role * HALF + i
    gaps = lanes(tab, 0, role, i) - across_ref[at : at + 1, :]
    return jnp.exp(jnp.where(rows >= cols, gaps, -jnp.inf))


def intra_kernel(
    role, core_ref, query_ref, keys_ref, value_ref, gate_ref, gain_ref, mixed_ref, tab_ref, across_ref,
    intra_ref, normed_ref,
):
    core = core_ref[0]
    tab = tab_ref[...]
    for i in range(HALF):
        at = columns(role, core, i)
        to = slice(i * DH, (i + 1) * DH)
        scores = dot(query_ref[:, at], keys_ref[:, at], 1, 1)
        probs = (scores * weights_of(tab, across_ref, role, i)).astype(BF16)
        intra_ref[:, to] = dot(probs, value_ref[:, at], 1, 0)
        opening = jax.nn.sigmoid(gate_ref[:, at].astype(F32))
        normed_ref[:, to] = mixed_ref[:, at].astype(F32) * opening * gain_ref[:, at]


def attend_kernel(role, core_ref, query_ref, state_ref, intra_ref, normed_ref, tab_ref, sums_ref, out_ref, add_ref):
    core = core_ref[0]
    tab = tab_ref[...]
    squares = jnp.zeros((GROUP, DH), F32)
    products = jnp.zeros((GROUP, DH), F32)
    for i in range(HALF):
        at = columns(role, core, i)
        to = slice(i * DH, (i + 1) * DH)
        inter = dot(query_ref[:, at], state_ref[i].astype(BF16), 1, 0)
        attention = intra_ref[:, to] + inter * lanes(tab, 1, role, i)
        out_ref[:, to] = attention
        squares = squares + attention * attention
        products = products + normed_ref[:, to] * attention
    ones = jnp.ones((8, DH), F32)
    squares = dot(ones, squares, 1, 1, lax.Precision.HIGHEST)
    products = dot(ones, products, 1, 1, lax.Precision.HIGHEST)
    row = lax.broadcasted_iota(jnp.int32, (8, GROUP), 0)
    both = jnp.where(row == 0, squares, products)
    add_ref[...] = both if sums_ref is None else sums_ref[...] + both


def upright(row):
    rows = lax.broadcasted_iota(jnp.int32, (GROUP, GROUP), 0)
    cols = lax.broadcasted_iota(jnp.int32, (GROUP, GROUP), 1)
    return jnp.sum(jnp.where(rows == cols, row, 0.0), axis=1, keepdims=True)


def norm_terms(sums_ref):
    scale = lax.rsqrt(sums_ref[0:1, :] / FEATURES + EPSILON)
    projection = scale * sums_ref[1:2, :] / FEATURES
    return upright(scale), upright(projection)


def grad_kernel(role, core_ref, query_ref, attention_ref, normed_ref, tab_ref, sums_ref, grad_ref, term_ref):
    core = core_ref[0]
    tab = tab_ref[...]
    scale, projection = norm_terms(sums_ref)
    for i in range(HALF):
        at = columns(role, core, i)
        to = slice(i * DH, (i + 1) * DH)
        normed = attention_ref[:, to] * scale
        grad = (scale * (normed_ref[:, to] - normed * projection)).astype(BF16)
        grad_ref[:, to] = grad
        weighted = (query_ref[:, at].astype(F32) * lanes(tab, 1, role, i)).astype(BF16)
        term_ref[i * DH : (i + 1) * DH, :] = dot(weighted, grad, 0, 0)


def inner_kernel(
    role, core_ref, query_ref, keys_ref, value_ref, state_ref, grad_ref, tab_ref, across_ref,
    query_out, keys_out, value_out,
):
    core = core_ref[0]
    tab = tab_ref[...]
    for i in range(HALF):
        at = columns(role, core, i)
        to = slice(i * DH, (i + 1) * DH)
        query, keys, value, grad = query_ref[:, at], keys_ref[:, at], value_ref[:, at], grad_ref[:, to]
        weights = weights_of(tab, across_ref, role, i)
        probs = (dot(query, keys, 1, 1) * weights).astype(BF16)
        grad_scores = (dot(grad, value, 1, 1) * weights).astype(BF16)
        grad_query = dot(grad_scores, keys, 1, 0)
        grad_query = grad_query + dot(grad, state_ref[i].astype(BF16), 1, 1) * lanes(tab, 1, role, i)
        query_out[:, to] = grad_query.astype(BF16)
        keys_out[:, to] = dot(grad_scores, query, 0, 0)
        value_out[:, to] = dot(probs, grad, 0, 0)


def gate_kernel(
    core_ref, gate_ref, gain_ref, upstream_ref, own_ref, other_ref, own_query, other_query, sums_ref,
    mixed_out, gate_out, query_out,
):
    core = core_ref[0]
    scale, _ = norm_terms(sums_ref)
    for role, ref, grad_query in ((0, own_ref, own_query), (1, other_ref, other_query)):
        for i in range(HALF):
            at = columns(role, core, i)
            to = slice(i * DH, (i + 1) * DH)
            shaped = ref[:, to] * scale * gain_ref[:, at]
            opening = jax.nn.sigmoid(gate_ref[:, at].astype(F32))
            mixed_out[:, at] = (shaped * opening).astype(BF16)
            upstream = upstream_ref[:, at].astype(F32)
            gate_out[:, at] = (upstream * shaped * opening * (1.0 - opening)).astype(BF16)
            query_out[:, at] = grad_query[:, to]


def last_kernel(
    role, core_ref, keys_ref, value_ref, state_ref, part_keys, part_value, tab_ref, *refs
):
    keys_out, value_out, keys_buf, value_buf, sems = refs[-5:]
    core = core_ref[0]
    tab = tab_ref[...]
    copies = []
    for i in range(HALF):
        at = columns(role, core, i)
        to = slice(i * DH, (i + 1) * DH)
        state = state_ref[i].astype(BF16)
        toward_end = lanes(tab, 2, role, i)
        grad_keys = part_keys[:, to] + dot(value_ref[:, at], state, 1, 1) * toward_end
        grad_value = part_value[:, to] + dot(keys_ref[:, at], state, 1, 0) * toward_end
        keys_buf[:, to] = grad_keys.astype(BF16)
        value_buf[:, to] = grad_value.astype(BF16)
        if i % 2 == 1:
            width = 2 * DH
            start = (i - 1) * DH
            side = core if role == 0 else 1 - core
            away = pl.ds(pl.multiple_of(side * WIDE + start, width), width)
            for buf, out in ((keys_buf, keys_out), (value_buf, value_out)):
                copy = pltpu.make_async_copy(buf.at[:, start : start + width], out.at[:, away], sems.at[len(copies)])
                copy.start()
                copies.append(copy)
    for copy in copies:
        copy.wait()


def swap(array):
    return lax.ppermute(array, "core", [(0, 1), (1, 0)])


def shifted(array, by):
    return lax.ppermute(array, "z1", [(i, i + by) for i in range(4) if 0 <= i + by < 4])


def spread(array):
    return lax.all_to_all(array, PLANE, 0, 0, tiled=True)


def across_heads(array):
    for flip in (1, 3):
        array = array + lax.ppermute(array, "head", [(i, i ^ flip) for i in range(4)])
    return array


def scan(core, own, other, tab, dec, decays, reverse, beside):
    if reverse:
        totals = call(merge_backward, shape(HALF, DH, DH), core, own, other, dec, name="merge_b")
    else:
        totals, dec = call(
            merge_forward, (shape(HALF, DH + 8, DH), shape(2 * HALF, DH)), core, own, other, tab, name="merge_f"
        )
    parts = spread(totals)
    decays = parts if decays is None else decays
    row = call(
        functools.partial(total_kernel, reverse), shape(DH + 8, DH), parts, decays, smem=0, name="row_total"
    )
    step = -1 if reverse else 1
    moved = [shifted(row, step * by) for by in (1, 2, 3)]
    (near, mid, far), beside = lax.optimization_barrier((moved, beside(row)))
    entering = call(
        functools.partial(enter_kernel, reverse), shape(8, DH, DH), parts, decays, near, mid, far, smem=0, name="enter"
    )
    entering = spread(entering)
    keep, send = call(
        functools.partial(leave_kernel, reverse),
        (shape(HALF, DH, DH), shape(HALF, DH, DH)),
        core, entering, own, other, dec, name="leave",
    )
    return keep, swap(send), dec, decays, beside


def on_device(query, keys, value, gate, decay, gain, upstream):
    core = lax.axis_index("core").astype(jnp.int32).reshape(1)
    gain = gain.reshape(1, -1)
    big = 2 * GROUP * GROUP * DH * HALF
    small = big // 2

    full = shape(GROUP, 2 * WIDE, dtype=BF16)
    tab, across, send, keys, value = call(
        first_kernel,
        (shape(GROUP, 128), shape(16, GROUP), shape(WIDE + 8, DH), full, full),
        core, *(pltpu.with_memory_space_constraint(a, pltpu.HBM) for a in (keys, value, decay.T)),
        flops=small, name="first",
        specs=[SMEM, HBM, HBM, HBM], scratch=[pltpu.VMEM((16, GROUP), F32), pltpu.SemaphoreType.DMA((5,))],
    )
    other = swap(send)
    own = call(second_kernel, shape(WIDE, DH), core, keys, value, tab, flops=small, name="second")

    wide = shape(GROUP, WIDE)

    def intra_parts(after):
        held, _ = lax.optimization_barrier((query, after))
        return [
            call(
                functools.partial(intra_kernel, role), (wide, wide),
                core, held, keys, value, gate, gain, upstream, tab, across, flops=2 * big, name=f"intra{role}",
            )
            for role in (0, 1)
        ]

    state_own, state_other, dec, decays, intra = scan(
        core, own, other, tab, None, None, False, intra_parts
    )

    def attend_first(core_ref, query_ref, state_ref, intra_ref, normed_ref, tab_ref, out_ref, add_ref):
        attend_kernel(0, core_ref, query_ref, state_ref, intra_ref, normed_ref, tab_ref, None, out_ref, add_ref)

    sums_shape = shape(8, GROUP)
    att_own, sums = call(
        attend_first, (wide, sums_shape), core, query, state_own, *intra[0], tab, flops=small, name="attend0"
    )
    att_other, sums = call(
        functools.partial(attend_kernel, 1), (wide, sums_shape),
        core, query, state_other, *intra[1], tab, sums, flops=small, name="attend1",
    )
    sums = across_heads(sums)

    grads_shape = (shape(GROUP, WIDE, dtype=BF16), shape(WIDE, DH))
    grad_other, term_send = call(
        functools.partial(grad_kernel, 1), grads_shape, core, query, att_other, intra[1][1], tab, sums,
        flops=small, name="grad1",
    )
    term_other = swap(term_send)
    grad_own, term_own = call(
        functools.partial(grad_kernel, 0), grads_shape, core, query, att_own, intra[0][1], tab, sums,
        flops=small, name="grad0",
    )

    def inner_parts(after):
        held, _ = lax.optimization_barrier((query, after))
        inner = [
            call(
                functools.partial(inner_kernel, role), (shape(GROUP, WIDE, dtype=BF16), wide, wide),
                core, held, keys, value, state, grad, tab, across, flops=6 * big, name=f"inner{role}",
            )
            for role, state, grad in ((0, state_own, grad_own), (1, state_other, grad_other))
        ]

        return inner, call(
            gate_kernel, (full, full, full),
            core, gate, gain, upstream, att_own, att_other, inner[0][0], inner[1][0], sums, name="gates", limit=20,
        )

    after_own, after_other, _, _, (inner, (mixed, grad_gate, grad_query)) = scan(
        core, term_own, term_other, tab, dec, decays, True, inner_parts
    )
    half = pltpu.VMEM((GROUP, WIDE), BF16)
    ends = ()
    for role, state in ((0, after_own), (1, after_other)):
        ends = call(
            functools.partial(last_kernel, role), (full, full),
            core, keys, value, state, *inner[role][1:], tab, *ends, flops=2 * small, name=f"last{role}",
            specs=[SMEM] + [VMEM] * 6 + [HBM] * len(ends), outs=(HBM, HBM),
            scratch=[half, half, pltpu.SemaphoreType.DMA((8,))], aliases={7: 0, 8: 1} if ends else None,
        )
    grad_keys, grad_value = ends
    return mixed, grad_query, grad_keys, grad_value, grad_gate


def solution(mesh):
    levels = Mesh(mesh.devices.reshape(4, 2, 4, 2, 4), ("z1", "z0", "y", "core", "head"))
    seq = ("z1", "z0", "y", "core")
    both = P(seq, "head")
    return jax.shard_map(
        on_device,
        mesh=levels,
        in_specs=(both, both, both, both, both, P("head"), both),
        out_specs=(both,) * 5,
        check_vma=False,
    )
```

```python
import functools
import math

import jax
import jax.numpy as jnp
from jax import lax
from jax.experimental import pallas as pl
from jax.experimental.pallas import tpu as pltpu
from jax.sharding import Mesh, PartitionSpec as P

DH = 128
GROUP = 256
HALF = 8
WIDE = HALF * DH
FEATURES = 64 * DH
EPSILON = 1e-06
F32 = jnp.float32
BF16 = jnp.bfloat16
PLANE = ("z0", "y")
VMEM = pl.BlockSpec(memory_space=pltpu.VMEM)
SMEM = pl.BlockSpec(memory_space=pltpu.SMEM)
HBM = pl.BlockSpec(memory_space=pltpu.HBM)


def call(kernel, out, *args, flops=0, smem=1, limit=6, name=None, specs=None, outs=None, scratch=(), aliases=None):
    moved = sum(a.size * a.dtype.itemsize for a in args)
    moved += sum(math.prod(o.shape) * 4 for o in jax.tree.leaves(out))
    return pl.pallas_call(
        kernel,
        out_shape=out,
        in_specs=specs or [SMEM] * smem + [VMEM] * (len(args) - smem),
        out_specs=outs or jax.tree.map(lambda _: VMEM, out),
        scratch_shapes=scratch,
        input_output_aliases=aliases or {},
        compiler_params=pltpu.CompilerParams(vmem_limit_bytes=limit << 20),
        cost_estimate=pl.CostEstimate(flops=flops, bytes_accessed=moved, transcendentals=0),
        name=name,
    )(*args)


def shape(*dims, dtype=F32):
    return jax.ShapeDtypeStruct(dims, dtype)


def dot(a, b, ca, cb, precision=None):
    return lax.dot_general(
        a, b, (((ca,), (cb,)), ((), ())), precision=precision, preferred_element_type=F32
    )


def columns(role, core, i):
    side = core if role == 0 else 1 - core
    return pl.ds(pl.multiple_of(side * WIDE + i * DH, DH), DH)


def lanes(tab, which, role, i):
    at = which * 16 + role * HALF + i
    return tab[:, at : at + 1]


def tables(core, decays):
    rows = lax.broadcasted_iota(jnp.int32, (GROUP, GROUP), 0)
    cols = lax.broadcasted_iota(jnp.int32, (GROUP, GROUP), 1)
    tri = (rows >= cols).astype(F32)
    down = dot(tri, decays, 1, 1, lax.Precision.HIGHEST)
    across = dot(decays, tri, 1, 1, lax.Precision.HIGHEST)
    swapped = jnp.concatenate([down[:, HALF:], down[:, :HALF]], axis=1)
    down = jnp.where(core == 0, down, swapped)
    across = jnp.where(core == 0, across, jnp.concatenate([across[HALF:], across[:HALF]], axis=0))
    return down, across


def state_term(core, role, i, keys_ref, value_ref, tab):
    at = columns(role, core, i)
    keyed = (keys_ref[:, at].astype(F32) * lanes(tab, 2, role, i)).astype(BF16)
    return dot(keyed, value_ref[:, at], 0, 0)


def first_kernel(
    core_ref, keys_hbm, value_hbm, decay_hbm, tab_ref, across_ref, send_ref, keys_ref, value_ref, decay_ref, sems
):
    core = core_ref[0]
    copies = [pltpu.make_async_copy(decay_hbm, decay_ref, sems.at[0])]
    for role in (1, 0):
        at = pl.ds(pl.multiple_of((core if role == 0 else 1 - core) * WIDE, WIDE), WIDE)
        for source, target in ((keys_hbm, keys_ref), (value_hbm, value_ref)):
            copies.append(pltpu.make_async_copy(source.at[:, at], target.at[:, at], sems.at[len(copies)]))
    for copy in copies:
        copy.start()
    copies[0].wait()
    down, across = tables(core, decay_ref[...])
    last = down[GROUP - 1 :, :]
    blank = jnp.zeros((GROUP, 128 - 48), F32)
    tab = jnp.concatenate([down, jnp.exp(down), jnp.exp(last - down), blank], axis=1)
    tab_ref[...] = tab
    across_ref[...] = across
    send_ref[WIDE:, :] = jnp.broadcast_to(tab[GROUP - 1 :, :], (8, 128))
    copies[1].wait()
    copies[2].wait()
    for i in range(HALF):
        send_ref[i * DH : (i + 1) * DH, :] = state_term(core, 1, i, keys_ref, value_ref, tab)
    copies[3].wait()
    copies[4].wait()


def second_kernel(core_ref, keys_ref, value_ref, tab_ref, keep_ref):
    core = core_ref[0]
    tab = tab_ref[...]
    for i in range(HALF):
        keep_ref[i * DH : (i + 1) * DH, :] = state_term(core, 0, i, keys_ref, value_ref, tab)


def merge_forward(core_ref, own_ref, other_ref, tab_ref, out_ref, dec_ref):
    zero = core_ref[0] == 0
    mine = tab_ref[GROUP - 1 :, :HALF]
    theirs = other_ref[WIDE : WIDE + 1, HALF : 2 * HALF]
    last_a = jnp.where(zero, mine, theirs)
    last_b = jnp.where(zero, theirs, mine)
    for i in range(HALF):
        own = own_ref[i * DH : (i + 1) * DH, :]
        other = other_ref[i * DH : (i + 1) * DH, :]
        a, b = jnp.where(zero, own, other), jnp.where(zero, other, own)
        here_a = jnp.broadcast_to(last_a[:, i : i + 1], (1, 128))
        here_b = jnp.broadcast_to(last_b[:, i : i + 1], (1, 128))
        dec_ref[i : i + 1, :] = jnp.exp(here_a)
        dec_ref[HALF + i : HALF + i + 1, :] = jnp.exp(here_b)
        out_ref[i, :DH, :] = jnp.exp(here_b) * a + b
        out_ref[i, DH:, :] = jnp.broadcast_to(here_a + here_b, (8, 128))


def merge_backward(core_ref, own_ref, other_ref, dec_ref, out_ref):
    zero = core_ref[0] == 0
    for i in range(HALF):
        own = own_ref[i * DH : (i + 1) * DH, :]
        other = other_ref[i * DH : (i + 1) * DH, :]
        a, b = jnp.where(zero, own, other), jnp.where(zero, other, own)
        out_ref[i] = a + dec_ref[i : i + 1, :] * b


def total_kernel(reverse, parts_ref, decays_ref, out_ref):
    order = list(range(8))[:: -1 if reverse else 1]
    total = parts_ref[order[0], :DH, :]
    for at in order[1:]:
        total = jnp.exp(decays_ref[at, DH : DH + 1, :]) * total + parts_ref[at, :DH, :]
    out_ref[:DH, :] = total
    decay = decays_ref[0, DH:, :]
    for at in range(1, 8):
        decay = decay + decays_ref[at, DH:, :]
    out_ref[DH:, :] = decay


def enter_kernel(reverse, place_ref, parts_ref, decays_ref, one_ref, two_ref, three_ref, out_ref):
    place = 3 - place_ref[0] if reverse else place_ref[0]
    one, two, three = one_ref[...], two_ref[...], three_ref[...]
    far = jnp.where(place >= 2, jnp.where(place == 2, two, three), 0.0)
    mid = jnp.where(place >= 2, jnp.where(place == 2, three, two), 0.0)
    near = jnp.where((place == 1) | (place == 3), one, 0.0)
    state = far[:DH, :]
    for part in (mid, near):
        state = jnp.exp(part[DH : DH + 1, :]) * state + part[:DH, :]
    order = list(range(8))[:: -1 if reverse else 1]
    for at in order:
        out_ref[at] = state
        if at != order[-1]:
            state = jnp.exp(decays_ref[at, DH : DH + 1, :]) * state + parts_ref[at, :DH, :]


def leave_kernel(reverse, core_ref, enter_ref, own_ref, other_ref, dec_ref, keep_ref, send_ref):
    first = core_ref[0] == (1 if reverse else 0)
    base = HALF if reverse else 0
    for i in range(HALF):
        own = own_ref[i * DH : (i + 1) * DH, :]
        other = other_ref[i * DH : (i + 1) * DH, :]
        nearer = jnp.where(first, own, other)
        x = enter_ref[i]
        y = dec_ref[base + i : base + i + 1, :] * x + nearer
        keep_ref[i] = jnp.where(first, x, y)
        send_ref[i] = jnp.where(first, y, x)


LOW, HIGH = slice(0, DH), slice(DH, GROUP)


def causal(low, first, second):
    return jnp.concatenate(
        [jnp.concatenate([low, jnp.zeros_like(low)], axis=1), jnp.concatenate([first, second], axis=1)], axis=0
    )


def intra_kernel(
    role, core_ref, query_ref, keys_ref, value_ref, gate_ref, gain_ref, mixed_ref, tab_ref, across_ref,
    intra_ref, normed_ref, probs_ref, weights_ref,
):
    core = core_ref[0]
    tab = tab_ref[...]
    rows = lax.broadcasted_iota(jnp.int32, (DH, DH), 0)
    cols = lax.broadcasted_iota(jnp.int32, (DH, DH), 1)
    lower = rows >= cols
    for i in range(HALF):
        at = columns(role, core, i)
        to = slice(i * DH, (i + 1) * DH)
        query, keys = query_ref[:, at], keys_ref[:, at]
        down = lanes(tab, 0, role, i)
        across = across_ref[role * HALF + i : role * HALF + i + 1, :]
        first = jnp.exp(jnp.where(lower, down[LOW] - across[:, LOW], -jnp.inf))
        second = jnp.exp(down[HIGH] - across[:, LOW])
        third = jnp.exp(jnp.where(lower, down[HIGH] - across[:, HIGH], -jnp.inf))
        weights_ref[i, 0], weights_ref[i, 1], weights_ref[i, 2] = first, second, third
        above = dot(query[LOW], keys[LOW], 1, 1)
        below = dot(query[HIGH], keys, 1, 1)
        probs = causal(
            (above * first).astype(BF16), (below[:, LOW] * second).astype(BF16), (below[:, HIGH] * third).astype(BF16)
        )
        probs_ref[i] = probs
        intra_ref[:, to] = dot(probs, value_ref[:, at], 1, 0)
        opening = jax.nn.sigmoid(gate_ref[:, at].astype(F32))
        normed_ref[:, to] = mixed_ref[:, at].astype(F32) * opening * gain_ref[:, at]


def attend_kernel(role, core_ref, query_ref, state_ref, intra_ref, normed_ref, tab_ref, sums_ref, out_ref, add_ref):
    core = core_ref[0]
    tab = tab_ref[...]
    squares = jnp.zeros((GROUP, DH), F32)
    products = jnp.zeros((GROUP, DH), F32)
    for i in range(HALF):
        at = columns(role, core, i)
        to = slice(i * DH, (i + 1) * DH)
        inter = dot(query_ref[:, at], state_ref[i].astype(BF16), 1, 0)
        attention = intra_ref[:, to] + inter * lanes(tab, 1, role, i)
        out_ref[:, to] = attention
        squares = squares + attention * attention
        products = products + normed_ref[:, to] * attention
    ones = jnp.ones((8, DH), F32)
    squares = dot(ones, squares, 1, 1, lax.Precision.HIGHEST)
    products = dot(ones, products, 1, 1, lax.Precision.HIGHEST)
    row = lax.broadcasted_iota(jnp.int32, (8, GROUP), 0)
    both = jnp.where(row == 0, squares, products)
    add_ref[...] = both if sums_ref is None else sums_ref[...] + both


def norm_terms(sums, terms_ref):
    scale = lax.rsqrt(sums[0:1, :] / FEATURES + EPSILON)
    projection = scale * sums[1:2, :] / FEATURES
    both = jnp.concatenate([scale, scale * projection, jnp.zeros((6, GROUP), F32)], axis=0)
    terms_ref[...] = jnp.concatenate([both.T, jnp.zeros((GROUP, DH - 8), F32)], axis=1)


def grad_kernel(role, core_ref, query_ref, attention_ref, normed_ref, tab_ref, terms_ref, grad_ref, term_ref):
    core = core_ref[0]
    tab = tab_ref[...]
    scale, shift = terms_ref[:, 0:1], terms_ref[:, 1:2]
    for i in range(HALF):
        at = columns(role, core, i)
        to = slice(i * DH, (i + 1) * DH)
        grad = (scale * (normed_ref[:, to] - attention_ref[:, to] * shift)).astype(BF16)
        grad_ref[:, to] = grad
        weighted = (query_ref[:, at].astype(F32) * lanes(tab, 1, role, i)).astype(BF16)
        term_ref[i * DH : (i + 1) * DH, :] = dot(weighted, grad, 0, 0)


def grad_first(
    core_ref, query_ref, attention_ref, normed_ref, tab_ref, sum_a, sum_b, sum_c, sum_d, grad_ref, term_ref, terms_ref
):
    norm_terms((sum_a[...] + sum_b[...]) + (sum_c[...] + sum_d[...]), terms_ref)
    grad_kernel(1, core_ref, query_ref, attention_ref, normed_ref, tab_ref, terms_ref, grad_ref, term_ref)


class Sender:
    def __init__(self, role, core, sems):
        self.side = core if role == 0 else 1 - core
        self.sems = sems
        self.copies = []

    def send(self, buf, out, start, width):
        away = pl.ds(pl.multiple_of(self.side * WIDE + start, width), width)
        copy = pltpu.make_async_copy(
            buf.at[:, start : start + width], out.at[:, away], self.sems.at[len(self.copies)]
        )
        copy.start()
        self.copies.append(copy)

    def wait(self):
        for copy in self.copies:
            copy.wait()


def inner_kernel(
    role, core_ref, query_ref, keys_ref, value_ref, state_ref, grad_ref, probs_ref, weights_ref, tab_ref, *refs
):
    query_out, keys_out, value_out, query_buf, sems = refs[-5:]
    core = core_ref[0]
    tab = tab_ref[...]
    sender = Sender(role, core, sems)
    for i in range(HALF):
        at = columns(role, core, i)
        to = slice(i * DH, (i + 1) * DH)
        query, keys, value, grad = query_ref[:, at], keys_ref[:, at], value_ref[:, at], grad_ref[:, to]
        above = dot(grad[LOW], value[LOW], 1, 1)
        below = dot(grad[HIGH], value, 1, 1)
        grad_scores = causal(
            (above * weights_ref[i, 0]).astype(BF16),
            (below[:, LOW] * weights_ref[i, 1]).astype(BF16),
            (below[:, HIGH] * weights_ref[i, 2]).astype(BF16),
        )
        grad_query = dot(grad_scores, keys, 1, 0)
        grad_query = grad_query + dot(grad, state_ref[i].astype(BF16), 1, 1) * lanes(tab, 1, role, i)
        query_buf[:, to] = grad_query.astype(BF16)
        keys_out[:, to] = dot(grad_scores, query, 0, 0)
        value_out[:, to] = dot(probs_ref[i], grad, 0, 0)
        if i % 2 == 1:
            sender.send(query_buf, query_out, (i - 1) * DH, 2 * DH)
    sender.wait()


def opened_kernel(
    core_ref, gate_ref, gain_ref, upstream_ref, own_ref, other_ref, own_normed, other_normed, mixed_ref, gate_out
):
    core = core_ref[0]
    for role, ref, normed_ref in ((0, own_ref, own_normed), (1, other_ref, other_normed)):
        for i in range(HALF):
            at = columns(role, core, i)
            to = slice(i * DH, (i + 1) * DH)
            into = slice(role * WIDE + i * DH, role * WIDE + (i + 1) * DH)
            opening = jax.nn.sigmoid(gate_ref[:, at].astype(F32))
            attention = ref[:, to]
            mixed_ref[:, into] = attention * (gain_ref[:, at] * opening)
            gate_out[:, into] = normed_ref[:, to] * (attention * (1.0 - opening))


def gate_kernel(core_ref, mixed_ref, gate_ref, terms_ref, mixed_out, gate_out, mixed_buf, gate_buf, sems):
    core = core_ref[0]
    scale = terms_ref[:, 0:1]
    for role in (0, 1):
        sender = Sender(role, core, sems.at[role])
        for i in range(HALF):
            into = slice(role * WIDE + i * DH, role * WIDE + (i + 1) * DH)
            mixed_buf[:, into] = (mixed_ref[:, into] * scale).astype(BF16)
            gate_buf[:, into] = (gate_ref[:, into] * scale).astype(BF16)
            if i % 4 == 3:
                start = role * WIDE + (i - 3) * DH
                for buf, out in ((mixed_buf, mixed_out), (gate_buf, gate_out)):
                    part = pl.ds(pl.multiple_of(sender.side * WIDE + (i - 3) * DH, 4 * DH), 4 * DH)
                    copy = pltpu.make_async_copy(
                        buf.at[:, start : start + 4 * DH], out.at[:, part], sems.at[role, len(sender.copies)]
                    )
                    copy.start()
                    sender.copies.append(copy)
        if role == 0:
            held = sender
    held.wait()
    sender.wait()


def last_kernel(
    role, core_ref, keys_ref, value_ref, state_ref, part_keys, part_value, tab_ref, *refs
):
    keys_out, value_out, keys_buf, value_buf, sems = refs[-5:]
    core = core_ref[0]
    tab = tab_ref[...]
    sender = Sender(role, core, sems)
    for i in range(HALF):
        at = columns(role, core, i)
        to = slice(i * DH, (i + 1) * DH)
        state = state_ref[i].astype(BF16)
        toward_end = lanes(tab, 2, role, i)
        grad_keys = part_keys[:, to] + dot(value_ref[:, at], state, 1, 1) * toward_end
        grad_value = part_value[:, to] + dot(keys_ref[:, at], state, 1, 0) * toward_end
        keys_buf[:, to] = grad_keys.astype(BF16)
        value_buf[:, to] = grad_value.astype(BF16)
        if i % 2 == 1:
            for buf, out in ((keys_buf, keys_out), (value_buf, value_out)):
                sender.send(buf, out, (i - 1) * DH, 2 * DH)
    sender.wait()


def swap(array):
    return lax.ppermute(array, "core", [(0, 1), (1, 0)])


def flipped(array, axis, flip):
    return lax.ppermute(array, axis, [(i, i ^ flip) for i in range(4)])


def spread(array):
    return lax.all_to_all(array, PLANE, 0, 0, tiled=True)


def scan(core, place, own, other, tab, dec, decays, reverse, beside):
    if reverse:
        totals = call(merge_backward, shape(HALF, DH, DH), core, own, other, dec, name="merge_b")
    else:
        totals, dec = call(
            merge_forward, (shape(HALF, DH + 8, DH), shape(2 * HALF, DH)), core, own, other, tab, name="merge_f"
        )
    parts = spread(totals)
    decays = parts if decays is None else decays
    row = call(
        functools.partial(total_kernel, reverse), shape(DH + 8, DH), parts, decays, smem=0, name="row_total"
    )
    moved = [flipped(row, "z1", flip) for flip in (1, 2, 3)]
    moved, beside = lax.optimization_barrier((moved, beside(row)))
    entering = call(
        functools.partial(enter_kernel, reverse), shape(8, DH, DH), place, parts, decays, *moved, name="enter"
    )
    entering = spread(entering)
    keep, send = call(
        functools.partial(leave_kernel, reverse),
        (shape(HALF, DH, DH), shape(HALF, DH, DH)),
        core, entering, own, other, dec, name="leave",
    )
    return keep, swap(send), dec, decays, beside


def on_device(query, keys, value, gate, decay, gain, upstream):
    core, place = lax.optimization_barrier(
        [lax.axis_index(axis).astype(jnp.int32).reshape(1) for axis in ("core", "z1")]
    )
    gain = gain.reshape(1, -1)
    big = 2 * GROUP * GROUP * DH * HALF
    small = big // 2

    full = shape(GROUP, 2 * WIDE, dtype=BF16)
    tab, across, send, keys, value = call(
        first_kernel,
        (shape(GROUP, 128), shape(16, GROUP), shape(WIDE + 8, DH), full, full),
        core, *(pltpu.with_memory_space_constraint(a, pltpu.HBM) for a in (keys, value, decay.T)),
        flops=small, name="first",
        specs=[SMEM, HBM, HBM, HBM], scratch=[pltpu.VMEM((16, GROUP), F32), pltpu.SemaphoreType.DMA((5,))],
    )
    other = swap(send)
    own = call(second_kernel, shape(WIDE, DH), core, keys, value, tab, flops=small, name="second")

    wide = shape(GROUP, WIDE)
    probs_shape = shape(HALF, GROUP, GROUP, dtype=BF16)
    weights_shape = shape(HALF, 3, DH, DH)

    def intra_parts(after):
        held, _ = lax.optimization_barrier((query, after))
        return [
            call(
                functools.partial(intra_kernel, role), (wide, wide, probs_shape, weights_shape),
                core, held, keys, value, gate, gain, upstream, tab, across, flops=2 * big, name=f"intra{role}",
            )
            for role in (0, 1)
        ]

    state_own, state_other, dec, decays, intra = scan(
        core, place, own, other, tab, None, None, False, intra_parts
    )

    def attend_first(core_ref, query_ref, state_ref, intra_ref, normed_ref, tab_ref, out_ref, add_ref):
        attend_kernel(0, core_ref, query_ref, state_ref, intra_ref, normed_ref, tab_ref, None, out_ref, add_ref)

    sums_shape = shape(8, GROUP)
    att_own, sums = call(
        attend_first, (wide, sums_shape), core, query, state_own, *intra[0][:2], tab, flops=small, name="attend0"
    )
    att_other, sums = call(
        functools.partial(attend_kernel, 1), (wide, sums_shape),
        core, query, state_other, *intra[1][:2], tab, sums, flops=small, name="attend1",
    )
    opened = call(
        opened_kernel, (shape(GROUP, 2 * WIDE), shape(GROUP, 2 * WIDE)),
        core, gate, gain, upstream, att_own, att_other, intra[0][1], intra[1][1], name="opened",
    )
    moved = [flipped(sums, "head", flip) for flip in (1, 2, 3)]
    moved, opened = lax.optimization_barrier((moved, opened))

    grads_shape = (shape(GROUP, WIDE, dtype=BF16), shape(WIDE, DH))
    grad_other, term_send, terms = call(
        grad_first, (*grads_shape, shape(GROUP, DH)),
        core, query, att_other, intra[1][1], tab, sums, *moved, flops=small, name="grad1",
    )
    term_other = swap(term_send)
    grad_own, term_own = call(
        functools.partial(grad_kernel, 0), grads_shape, core, query, att_own, intra[0][1], tab, terms,
        flops=small, name="grad0",
    )

    def inner_parts(after):
        held, factors, _ = lax.optimization_barrier((query, terms, after))
        inner, queries = [], ()
        for role, state, grad in ((0, state_own, grad_own), (1, state_other, grad_other)):
            results = call(
                functools.partial(inner_kernel, role), (pltpu.HBM((GROUP, 2 * WIDE), BF16), wide, wide),
                core, held, keys, value, state, grad, *intra[role][2:], tab, *queries,
                flops=5 * big, name=f"inner{role}",
                specs=[SMEM] + [VMEM] * 8 + [HBM] * len(queries), outs=(HBM, VMEM, VMEM),
                scratch=[pltpu.VMEM((GROUP, WIDE), BF16), pltpu.SemaphoreType.DMA((4,))],
                aliases={9: 0} if queries else None,
            )
            queries = results[:1]
            inner.append(results[1:])
        whole = pltpu.VMEM((GROUP, 2 * WIDE), BF16)
        return inner, queries[0], call(
            gate_kernel, (full, full), core, *opened, factors, name="gates", outs=(HBM, HBM),
            scratch=[whole, whole, pltpu.SemaphoreType.DMA((2, 4))],
        )

    after_own, after_other, _, _, (inner, grad_query, (mixed, grad_gate)) = scan(
        core, place, term_own, term_other, tab, dec, decays, True, inner_parts
    )
    half = pltpu.VMEM((GROUP, WIDE), BF16)
    ends = ()
    for role, state in ((0, after_own), (1, after_other)):
        ends = call(
            functools.partial(last_kernel, role), (full, full),
            core, keys, value, state, *inner[role], tab, *ends, flops=2 * small, name=f"last{role}",
            specs=[SMEM] + [VMEM] * 6 + [HBM] * len(ends), outs=(HBM, HBM),
            scratch=[half, half, pltpu.SemaphoreType.DMA((8,))], aliases={7: 0, 8: 1} if ends else None,
        )
    grad_keys, grad_value = ends
    return mixed, grad_query, grad_keys, grad_value, grad_gate


def solution(mesh):
    levels = Mesh(mesh.devices.reshape(4, 2, 4, 2, 4), ("z1", "z0", "y", "core", "head"))
    seq = ("z1", "z0", "y", "core")
    both = P(seq, "head")
    return jax.shard_map(
        on_device,
        mesh=levels,
        in_specs=(both, both, both, both, both, P("head"), both),
        out_specs=(both,) * 5,
        check_vma=False,
    )
```

```python
import functools
import math

import jax
import jax.numpy as jnp
from jax import lax
from jax.experimental import pallas as pl
from jax.experimental.pallas import tpu as pltpu
from jax.sharding import Mesh, PartitionSpec as P

DH = 128
GROUP = 256
HALF = 8
WIDE = HALF * DH
FEATURES = 64 * DH
EPSILON = 1e-06
F32 = jnp.float32
BF16 = jnp.bfloat16
PLANE = ("z0", "y")
VMEM = pl.BlockSpec(memory_space=pltpu.VMEM)
SMEM = pl.BlockSpec(memory_space=pltpu.SMEM)
HBM = pl.BlockSpec(memory_space=pltpu.HBM)


def call(kernel, out, *args, flops=0, smem=1, limit=6, name=None, specs=None, outs=None, scratch=(), aliases=None):
    moved = sum(a.size * a.dtype.itemsize for a in args)
    moved += sum(math.prod(o.shape) * 4 for o in jax.tree.leaves(out))
    return pl.pallas_call(
        kernel,
        out_shape=out,
        in_specs=specs or [SMEM] * smem + [VMEM] * (len(args) - smem),
        out_specs=outs or jax.tree.map(lambda _: VMEM, out),
        scratch_shapes=scratch,
        input_output_aliases=aliases or {},
        compiler_params=pltpu.CompilerParams(vmem_limit_bytes=limit << 20),
        cost_estimate=pl.CostEstimate(flops=flops, bytes_accessed=moved, transcendentals=0),
        name=name,
    )(*args)


def shape(*dims, dtype=F32):
    return jax.ShapeDtypeStruct(dims, dtype)


def dot(a, b, ca, cb, precision=None):
    return lax.dot_general(
        a, b, (((ca,), (cb,)), ((), ())), precision=precision, preferred_element_type=F32
    )


def turned(x):
    n = x.shape[1]
    rows = lax.broadcasted_iota(jnp.int32, (n, n), 0)
    cols = lax.broadcasted_iota(jnp.int32, (n, n), 1)
    return dot((rows == cols).astype(BF16), x, 1, 1).astype(BF16)


def columns(role, core, i):
    side = core if role == 0 else 1 - core
    return pl.ds(pl.multiple_of(side * WIDE + i * DH, DH), DH)


def lanes(tab, which, role, i):
    at = which * 16 + role * HALF + i
    return tab[:, at : at + 1]


def tables(core, decays):
    rows = lax.broadcasted_iota(jnp.int32, (GROUP, GROUP), 0)
    cols = lax.broadcasted_iota(jnp.int32, (GROUP, GROUP), 1)
    tri = (rows >= cols).astype(BF16)
    high = decays.astype(BF16)
    rest = decays - high.astype(F32)
    middle = rest.astype(BF16)
    low = (rest - middle.astype(F32)).astype(BF16)
    across = dot(jnp.concatenate([high, middle, low], axis=0), tri, 1, 1)
    across = across[:16] + (across[16:32] + across[32:])
    across = jnp.where(core == 0, across, jnp.concatenate([across[HALF:], across[:HALF]], axis=0))
    return across.T, across


def state_term(core, role, i, keys_ref, value_ref, tab):
    at = columns(role, core, i)
    keyed = (keys_ref[:, at].astype(F32) * lanes(tab, 2, role, i)).astype(BF16)
    return dot(turned(keyed), value_ref[:, at], 1, 0)


def first_kernel(
    core_ref, keys_hbm, value_hbm, decay_hbm, tab_ref, across_ref, send_ref, keys_ref, value_ref, decay_ref, sems
):
    core = core_ref[0]
    copies = [pltpu.make_async_copy(decay_hbm, decay_ref, sems.at[0])]
    for role in (1, 0):
        at = pl.ds(pl.multiple_of((core if role == 0 else 1 - core) * WIDE, WIDE), WIDE)
        for source, target in ((keys_hbm, keys_ref), (value_hbm, value_ref)):
            copies.append(pltpu.make_async_copy(source.at[:, at], target.at[:, at], sems.at[len(copies)]))
    for copy in copies:
        copy.start()
    copies[0].wait()
    down, across = tables(core, decay_ref[...])
    last = down[GROUP - 1 :, :]
    blank = jnp.zeros((GROUP, 128 - 48), F32)
    tab = jnp.concatenate([down, jnp.exp(down), jnp.exp(last - down), blank], axis=1)
    tab_ref[...] = tab
    across_ref[...] = across
    send_ref[WIDE:, :] = jnp.broadcast_to(tab[GROUP - 1 :, :], (8, 128))
    copies[1].wait()
    copies[2].wait()
    for i in range(HALF):
        send_ref[i * DH : (i + 1) * DH, :] = state_term(core, 1, i, keys_ref, value_ref, tab)
    copies[3].wait()
    copies[4].wait()


def second_kernel(core_ref, keys_ref, value_ref, tab_ref, keep_ref):
    core = core_ref[0]
    tab = tab_ref[...]
    for i in range(HALF):
        keep_ref[i * DH : (i + 1) * DH, :] = state_term(core, 0, i, keys_ref, value_ref, tab)


def merge_forward(core_ref, own_ref, other_ref, tab_ref, out_ref, dec_ref):
    zero = core_ref[0] == 0
    mine = tab_ref[GROUP - 1 :, :HALF]
    theirs = other_ref[WIDE : WIDE + 1, HALF : 2 * HALF]
    last_a = jnp.where(zero, mine, theirs)
    last_b = jnp.where(zero, theirs, mine)
    for i in range(HALF):
        own = own_ref[i * DH : (i + 1) * DH, :]
        other = other_ref[i * DH : (i + 1) * DH, :]
        a, b = jnp.where(zero, own, other), jnp.where(zero, other, own)
        here_a = jnp.broadcast_to(last_a[:, i : i + 1], (1, 128))
        here_b = jnp.broadcast_to(last_b[:, i : i + 1], (1, 128))
        dec_ref[i : i + 1, :] = jnp.exp(here_a)
        dec_ref[HALF + i : HALF + i + 1, :] = jnp.exp(here_b)
        out_ref[i, :DH, :] = jnp.exp(here_b) * a + b
        out_ref[i, DH:, :] = jnp.broadcast_to(here_a + here_b, (8, 128))


def merge_backward(core_ref, own_ref, other_ref, dec_ref, out_ref):
    zero = core_ref[0] == 0
    for i in range(HALF):
        own = own_ref[i * DH : (i + 1) * DH, :]
        other = other_ref[i * DH : (i + 1) * DH, :]
        a, b = jnp.where(zero, own, other), jnp.where(zero, other, own)
        out_ref[i] = a + dec_ref[i : i + 1, :] * b


def total_kernel(reverse, parts_ref, decays_ref, out_ref):
    order = list(range(8))[:: -1 if reverse else 1]
    total = parts_ref[order[0], :DH, :]
    for at in order[1:]:
        total = jnp.exp(decays_ref[at, DH : DH + 1, :]) * total + parts_ref[at, :DH, :]
    out_ref[:DH, :] = total
    decay = decays_ref[0, DH:, :]
    for at in range(1, 8):
        decay = decay + decays_ref[at, DH:, :]
    out_ref[DH:, :] = decay


def enter_kernel(reverse, place_ref, parts_ref, decays_ref, one_ref, two_ref, three_ref, out_ref):
    place = 3 - place_ref[0] if reverse else place_ref[0]
    one, two, three = one_ref[...], two_ref[...], three_ref[...]
    far = jnp.where(place >= 2, jnp.where(place == 2, two, three), 0.0)
    mid = jnp.where(place >= 2, jnp.where(place == 2, three, two), 0.0)
    near = jnp.where((place == 1) | (place == 3), one, 0.0)
    state = far[:DH, :]
    for part in (mid, near):
        state = jnp.exp(part[DH : DH + 1, :]) * state + part[:DH, :]
    order = list(range(8))[:: -1 if reverse else 1]
    for at in order:
        out_ref[at] = state
        if at != order[-1]:
            state = jnp.exp(decays_ref[at, DH : DH + 1, :]) * state + parts_ref[at, :DH, :]


def leave_kernel(reverse, core_ref, enter_ref, own_ref, other_ref, dec_ref, keep_ref, send_ref):
    first = core_ref[0] == (1 if reverse else 0)
    base = HALF if reverse else 0
    for i in range(HALF):
        own = own_ref[i * DH : (i + 1) * DH, :]
        other = other_ref[i * DH : (i + 1) * DH, :]
        nearer = jnp.where(first, own, other)
        x = enter_ref[i]
        y = dec_ref[base + i : base + i + 1, :] * x + nearer
        keep_ref[i] = jnp.where(first, x, y)
        send_ref[i] = jnp.where(first, y, x)


LOW, HIGH = slice(0, DH), slice(DH, GROUP)


def causal(first, middle, last, upper=False):
    blank = jnp.zeros_like(first)
    top, bottom = ([first, middle], [blank, last]) if upper else ([first, blank], [middle, last])
    return jnp.concatenate([jnp.concatenate(top, axis=1), jnp.concatenate(bottom, axis=1)], axis=0)


def masked(array, weights, upper=False):
    middle = array[LOW, HIGH] if upper else array[HIGH, LOW]
    parts = (array[LOW, LOW], middle, array[HIGH, HIGH])
    return causal(*((part * weights[at]).astype(BF16) for at, part in enumerate(parts)), upper=upper)


def intra_kernel(
    role, core_ref, query_ref, keys_ref, value_ref, gate_ref, gain_ref, mixed_ref, tab_ref, across_ref,
    intra_ref, normed_ref, turned_ref, weights_ref,
):
    core = core_ref[0]
    tab = tab_ref[...]
    rows = lax.broadcasted_iota(jnp.int32, (DH, DH), 0)
    cols = lax.broadcasted_iota(jnp.int32, (DH, DH), 1)
    lower, upper = rows >= cols, rows <= cols
    for i in range(HALF):
        at = columns(role, core, i)
        to = slice(i * DH, (i + 1) * DH)
        query, keys = query_ref[:, at], keys_ref[:, at]
        down = lanes(tab, 0, role, i)
        across = across_ref[role * HALF + i : role * HALF + i + 1, :]
        weights = (
            jnp.exp(jnp.where(lower, down[LOW] - across[:, LOW], -jnp.inf)),
            jnp.exp(down[HIGH] - across[:, LOW]),
            jnp.exp(jnp.where(lower, down[HIGH] - across[:, HIGH], -jnp.inf)),
            jnp.exp(jnp.where(upper, across[:, LOW] - down[LOW], -jnp.inf)),
            jnp.exp(across[:, HIGH] - down[LOW]),
            jnp.exp(jnp.where(upper, across[:, HIGH] - down[HIGH], -jnp.inf)),
        )
        for part, array in enumerate(weights):
            weights_ref[i, part] = array
        probs = masked(dot(query, keys, 1, 1), weights[:3])
        turned_ref[i] = masked(dot(keys, query, 1, 1), weights[3:], upper=True)
        intra_ref[:, to] = dot(probs, value_ref[:, at], 1, 0)
        opening = jax.nn.sigmoid(gate_ref[:, at].astype(F32))
        normed_ref[:, to] = mixed_ref[:, at].astype(F32) * opening * gain_ref[:, at]


def attend_kernel(role, core_ref, query_ref, state_ref, intra_ref, normed_ref, tab_ref, *refs):
    if role == 0:
        out_ref, squares_ref, products_ref = refs
        squares, products = jnp.zeros((GROUP, DH), F32), jnp.zeros((GROUP, DH), F32)
    else:
        squares_in, products_in, out_ref, sums_ref = refs
        squares, products = squares_in[...], products_in[...]
    core = core_ref[0]
    tab = tab_ref[...]
    for i in range(HALF):
        at = columns(role, core, i)
        to = slice(i * DH, (i + 1) * DH)
        inter = dot(query_ref[:, at], state_ref[i].astype(BF16), 1, 0)
        attention = intra_ref[:, to] + inter * lanes(tab, 1, role, i)
        out_ref[:, to] = attention
        squares = squares + attention * attention
        products = products + normed_ref[:, to] * attention
    if role == 0:
        squares_ref[...] = squares
        products_ref[...] = products
    else:
        both = [jnp.sum(array.T, axis=0, keepdims=True) for array in (squares, products)]
        sums_ref[...] = jnp.concatenate(both + [jnp.zeros((6, GROUP), F32)], axis=0)


def norm_terms(sums, terms_ref):
    scale = lax.rsqrt(sums[0:1, :] / FEATURES + EPSILON)
    projection = scale * sums[1:2, :] / FEATURES
    both = jnp.concatenate([scale, scale * projection, jnp.zeros((6, GROUP), F32)], axis=0)
    terms_ref[...] = jnp.concatenate([both.T, jnp.zeros((GROUP, DH - 8), F32)], axis=1)


def grad_kernel(role, core_ref, query_ref, attention_ref, normed_ref, tab_ref, terms_ref, grad_ref, term_ref):
    core = core_ref[0]
    tab = tab_ref[...]
    scale, shift = terms_ref[:, 0:1], terms_ref[:, 1:2]
    for i in range(HALF):
        at = columns(role, core, i)
        to = slice(i * DH, (i + 1) * DH)
        grad = (scale * (normed_ref[:, to] - attention_ref[:, to] * shift)).astype(BF16)
        grad_ref[:, to] = grad
        weighted = (query_ref[:, at].astype(F32) * lanes(tab, 1, role, i)).astype(BF16)
        term_ref[i * DH : (i + 1) * DH, :] = dot(turned(weighted), grad, 1, 0)


def grad_first(
    core_ref, query_ref, attention_ref, normed_ref, tab_ref, sum_a, sum_b, sum_c, sum_d, grad_ref, term_ref, terms_ref
):
    norm_terms((sum_a[...] + sum_b[...]) + (sum_c[...] + sum_d[...]), terms_ref)
    grad_kernel(1, core_ref, query_ref, attention_ref, normed_ref, tab_ref, terms_ref, grad_ref, term_ref)


class Sender:
    def __init__(self, role, core, sems):
        self.side = core if role == 0 else 1 - core
        self.sems = sems
        self.copies = []

    def send(self, buf, out, start, width):
        away = pl.ds(pl.multiple_of(self.side * WIDE + start, width), width)
        copy = pltpu.make_async_copy(
            buf.at[:, start : start + width], out.at[:, away], self.sems.at[len(self.copies)]
        )
        copy.start()
        self.copies.append(copy)

    def wait(self):
        for copy in self.copies:
            copy.wait()


def inner_part(
    role, core, query_ref, keys_ref, value_ref, state_ref, grad_ref, turned_ref, weights_ref, tab, keys_out, value_out,
    query_buf, sender, query_out,
):
    for i in range(HALF):
        at = columns(role, core, i)
        to = slice(i * DH, (i + 1) * DH)
        query, keys, value, grad = query_ref[:, at], keys_ref[:, at], value_ref[:, at], grad_ref[:, to]
        weights = [weights_ref[i, part] for part in range(6)]
        scores = masked(dot(grad, value, 1, 1), weights[:3])
        flipped_scores = masked(dot(value, grad, 1, 1), weights[3:], upper=True)
        grad_query = dot(scores, keys, 1, 0)
        grad_query = grad_query + dot(grad, state_ref[i].astype(BF16), 1, 1) * lanes(tab, 1, role, i)
        query_buf[:, to] = grad_query.astype(BF16)
        keys_out[:, to] = dot(flipped_scores, query, 1, 0)
        value_out[:, to] = dot(turned_ref[i], grad, 1, 0)
        if i % 2 == 1:
            sender.send(query_buf, query_out, (i - 1) * DH, 2 * DH)


def local_kernel(
    core_ref, query_ref, keys_ref, value_ref, own_state, other_state, own_grad, other_grad, own_turned, own_weights,
    other_turned, other_weights, tab_ref, mixed_ref, gate_ref, terms_ref,
    query_out, mixed_out, gate_out, own_keys, own_value, other_keys, other_value,
    query_own, query_other, mixed_own, mixed_other, gate_own, gate_other, sems,
):
    core = core_ref[0]
    tab = tab_ref[...]
    scale = terms_ref[:, 0:1]
    senders = [Sender(role, core, sems.at[role]) for role in (0, 1)]

    def gates(role, mixed_buf, gate_buf):
        for i in range(HALF):
            to = slice(i * DH, (i + 1) * DH)
            into = slice(role * WIDE + i * DH, role * WIDE + (i + 1) * DH)
            mixed_buf[:, to] = (mixed_ref[:, into] * scale).astype(BF16)
            gate_buf[:, to] = (gate_ref[:, into] * scale).astype(BF16)
            if i % 4 == 3:
                senders[role].send(mixed_buf, mixed_out, (i - 3) * DH, 4 * DH)
                senders[role].send(gate_buf, gate_out, (i - 3) * DH, 4 * DH)

    gates(0, mixed_own, gate_own)
    gates(1, mixed_other, gate_other)
    inner_part(
        0, core, query_ref, keys_ref, value_ref, own_state, own_grad, own_turned, own_weights, tab, own_keys, own_value,
        query_own, senders[0], query_out,
    )
    inner_part(
        1, core, query_ref, keys_ref, value_ref, other_state, other_grad, other_turned, other_weights, tab, other_keys,
        other_value, query_other, senders[1], query_out,
    )
    for sender in senders:
        sender.wait()


def opened_kernel(
    core_ref, gate_ref, gain_ref, upstream_ref, own_ref, other_ref, own_normed, other_normed, mixed_ref, gate_out
):
    core = core_ref[0]
    for role, ref, normed_ref in ((0, own_ref, own_normed), (1, other_ref, other_normed)):
        for i in range(HALF):
            at = columns(role, core, i)
            to = slice(i * DH, (i + 1) * DH)
            into = slice(role * WIDE + i * DH, role * WIDE + (i + 1) * DH)
            opening = jax.nn.sigmoid(gate_ref[:, at].astype(F32))
            attention = ref[:, to]
            mixed_ref[:, into] = attention * (gain_ref[:, at] * opening)
            gate_out[:, into] = normed_ref[:, to] * (attention * (1.0 - opening))


def last_kernel(
    role, core_ref, keys_ref, value_ref, state_ref, part_keys, part_value, tab_ref, *refs
):
    keys_out, value_out, keys_buf, value_buf, sems = refs[-5:]
    core = core_ref[0]
    tab = tab_ref[...]
    sender = Sender(role, core, sems)
    for i in range(HALF):
        at = columns(role, core, i)
        to = slice(i * DH, (i + 1) * DH)
        state = state_ref[i].astype(BF16)
        toward_end = lanes(tab, 2, role, i)
        grad_keys = part_keys[:, to] + dot(value_ref[:, at], state, 1, 1) * toward_end
        grad_value = part_value[:, to] + dot(keys_ref[:, at], state, 1, 0) * toward_end
        keys_buf[:, to] = grad_keys.astype(BF16)
        value_buf[:, to] = grad_value.astype(BF16)
        if i % 2 == 1:
            for buf, out in ((keys_buf, keys_out), (value_buf, value_out)):
                sender.send(buf, out, (i - 1) * DH, 2 * DH)
    sender.wait()


def swap(array):
    return lax.ppermute(array, "core", [(0, 1), (1, 0)])


def flipped(array, axis, flip):
    return lax.ppermute(array, axis, [(i, i ^ flip) for i in range(4)])


def spread(array):
    return lax.all_to_all(array, PLANE, 0, 0, tiled=True)


def scan(core, place, own, other, tab, dec, decays, reverse, beside):
    if reverse:
        totals = call(merge_backward, shape(HALF, DH, DH), core, own, other, dec, name="merge_b")
    else:
        totals, dec = call(
            merge_forward, (shape(HALF, DH + 8, DH), shape(2 * HALF, DH)), core, own, other, tab, name="merge_f"
        )
    parts = spread(totals)
    decays = parts if decays is None else decays
    row = call(
        functools.partial(total_kernel, reverse), shape(DH + 8, DH), parts, decays, smem=0, name="row_total"
    )
    moved = [flipped(row, "z1", flip) for flip in (1, 2, 3)]
    moved, beside = lax.optimization_barrier((moved, beside(row)))
    entering = call(
        functools.partial(enter_kernel, reverse), shape(8, DH, DH), place, parts, decays, *moved, name="enter"
    )
    entering = spread(entering)
    keep, send = call(
        functools.partial(leave_kernel, reverse),
        (shape(HALF, DH, DH), shape(HALF, DH, DH)),
        core, entering, own, other, dec, name="leave",
    )
    return keep, swap(send), dec, decays, beside


def on_device(query, keys, value, gate, decay, gain, upstream):
    core, place = lax.optimization_barrier(
        [lax.axis_index(axis).astype(jnp.int32).reshape(1) for axis in ("core", "z1")]
    )
    gain = gain.reshape(1, -1)
    big = 2 * GROUP * GROUP * DH * HALF
    small = big // 2

    full = shape(GROUP, 2 * WIDE, dtype=BF16)
    tab, across, send, keys, value = call(
        first_kernel,
        (shape(GROUP, 128), shape(16, GROUP), shape(WIDE + 8, DH), full, full),
        core, *(pltpu.with_memory_space_constraint(a, pltpu.HBM) for a in (keys, value, decay.T)),
        flops=small, name="first",
        specs=[SMEM, HBM, HBM, HBM], scratch=[pltpu.VMEM((16, GROUP), F32), pltpu.SemaphoreType.DMA((5,))],
    )
    other = swap(send)
    own = call(second_kernel, shape(WIDE, DH), core, keys, value, tab, flops=small, name="second")

    wide = shape(GROUP, WIDE)
    probs_shape = shape(HALF, GROUP, GROUP, dtype=BF16)
    weights_shape = shape(HALF, 6, DH, DH)

    def intra_parts(after):
        held, _ = lax.optimization_barrier((query, after))
        return [
            call(
                functools.partial(intra_kernel, role), (wide, wide, probs_shape, weights_shape),
                core, held, keys, value, gate, gain, upstream, tab, across, flops=2 * big, name=f"intra{role}",
            )
            for role in (0, 1)
        ]

    state_own, state_other, dec, decays, intra = scan(
        core, place, own, other, tab, None, None, False, intra_parts
    )

    narrow = shape(GROUP, DH)
    att_own, *partial = call(
        functools.partial(attend_kernel, 0), (wide, narrow, narrow),
        core, query, state_own, *intra[0][:2], tab, flops=small, name="attend0",
    )
    att_other, sums = call(
        functools.partial(attend_kernel, 1), (wide, shape(8, GROUP)),
        core, query, state_other, *intra[1][:2], tab, *partial, flops=small, name="attend1",
    )
    opened = call(
        opened_kernel, (shape(GROUP, 2 * WIDE), shape(GROUP, 2 * WIDE)),
        core, gate, gain, upstream, att_own, att_other, intra[0][1], intra[1][1], name="opened",
    )
    moved = [flipped(sums, "head", flip) for flip in (1, 2, 3)]
    moved, opened = lax.optimization_barrier((moved, opened))

    grads_shape = (shape(GROUP, WIDE, dtype=BF16), shape(WIDE, DH))
    grad_other, term_send, terms = call(
        grad_first, (*grads_shape, shape(GROUP, DH)),
        core, query, att_other, intra[1][1], tab, sums, *moved, flops=small, name="grad1",
    )
    term_other = swap(term_send)
    grad_own, term_own = call(
        functools.partial(grad_kernel, 0), grads_shape, core, query, att_own, intra[0][1], tab, terms,
        flops=small, name="grad0",
    )

    half = pltpu.VMEM((GROUP, WIDE), BF16)

    def local(after):
        held, factors, _ = lax.optimization_barrier((query, terms, after))
        return call(
            local_kernel, (full, full, full, wide, wide, wide, wide),
            core, held, keys, value, state_own, state_other, grad_own, grad_other, *intra[0][2:], *intra[1][2:], tab,
            *opened, factors, flops=10 * big, name="local", limit=14,
            outs=(HBM, HBM, HBM, VMEM, VMEM, VMEM, VMEM), scratch=[half] * 6 + [pltpu.SemaphoreType.DMA((2, 8))],
        )

    after_own, after_other, _, _, (grad_query, mixed, grad_gate, *inner) = scan(
        core, place, term_own, term_other, tab, dec, decays, True, local
    )
    ends = ()
    for role, state in ((0, after_own), (1, after_other)):
        ends = call(
            functools.partial(last_kernel, role), (full, full),
            core, keys, value, state, *inner[2 * role : 2 * role + 2], tab, *ends, flops=2 * small, name=f"last{role}",
            specs=[SMEM] + [VMEM] * 6 + [HBM] * len(ends), outs=(HBM, HBM),
            scratch=[half, half, pltpu.SemaphoreType.DMA((8,))], aliases={7: 0, 8: 1} if ends else None,
        )
    grad_keys, grad_value = ends
    return mixed, grad_query, grad_keys, grad_value, grad_gate


def solution(mesh):
    levels = Mesh(mesh.devices.reshape(4, 2, 4, 2, 4), ("z1", "z0", "y", "core", "head"))
    seq = ("z1", "z0", "y", "core")
    both = P(seq, "head")
    return jax.shard_map(
        on_device,
        mesh=levels,
        in_specs=(both, both, both, both, both, P("head"), both),
        out_specs=(both,) * 5,
        check_vma=False,
    )
```

```python
import functools
import math

import jax
import jax.numpy as jnp
from jax import lax
from jax.experimental import pallas as pl
from jax.experimental.pallas import tpu as pltpu
from jax.sharding import Mesh, PartitionSpec as P

DH = 128
GROUP = 256
HALF = 8
WIDE = HALF * DH
FEATURES = 64 * DH
EPSILON = 1e-06
F32 = jnp.float32
BF16 = jnp.bfloat16
PLANE = ("z0", "y")
VMEM = pl.BlockSpec(memory_space=pltpu.VMEM)
SMEM = pl.BlockSpec(memory_space=pltpu.SMEM)
HBM = pl.BlockSpec(memory_space=pltpu.HBM)


def call(kernel, out, *args, flops=0, smem=1, limit=6, name=None, specs=None, outs=None, scratch=(), aliases=None):
    moved = sum(a.size * a.dtype.itemsize for a in args)
    moved += sum(math.prod(o.shape) * 4 for o in jax.tree.leaves(out))
    return pl.pallas_call(
        kernel,
        out_shape=out,
        in_specs=specs or [SMEM] * smem + [VMEM] * (len(args) - smem),
        out_specs=outs or jax.tree.map(lambda _: VMEM, out),
        scratch_shapes=scratch,
        input_output_aliases=aliases or {},
        compiler_params=pltpu.CompilerParams(vmem_limit_bytes=limit << 20),
        cost_estimate=pl.CostEstimate(flops=flops, bytes_accessed=moved, transcendentals=0),
        name=name,
    )(*args)


def shape(*dims, dtype=F32):
    return jax.ShapeDtypeStruct(dims, dtype)


def dot(a, b, ca, cb, precision=None):
    return lax.dot_general(
        a, b, (((ca,), (cb,)), ((), ())), precision=precision, preferred_element_type=F32
    )


def turned(x):
    n = x.shape[1]
    rows = lax.broadcasted_iota(jnp.int32, (n, n), 0)
    cols = lax.broadcasted_iota(jnp.int32, (n, n), 1)
    return dot((rows == cols).astype(BF16), x, 1, 1).astype(BF16)


def columns(role, core, i):
    side = core if role == 0 else 1 - core
    return pl.ds(pl.multiple_of(side * WIDE + i * DH, DH), DH)


def lanes(tab, which, role, i):
    at = which * 16 + role * HALF + i
    return tab[:, at : at + 1]


def tables(core, decays):
    rows = lax.broadcasted_iota(jnp.int32, (GROUP, GROUP), 0)
    cols = lax.broadcasted_iota(jnp.int32, (GROUP, GROUP), 1)
    tri = (rows >= cols).astype(BF16)
    high = decays.astype(BF16)
    rest = decays - high.astype(F32)
    middle = rest.astype(BF16)
    low = (rest - middle.astype(F32)).astype(BF16)
    across = dot(jnp.concatenate([high, middle, low], axis=0), tri, 1, 1)
    across = across[:16] + (across[16:32] + across[32:])
    across = jnp.where(core == 0, across, jnp.concatenate([across[HALF:], across[:HALF]], axis=0))
    return across.T, across


def state_term(core, role, i, keys_ref, value_ref, tab):
    at = columns(role, core, i)
    keyed = (keys_ref[:, at].astype(F32) * lanes(tab, 2, role, i)).astype(BF16)
    return dot(turned(keyed), value_ref[:, at], 1, 0)


def first_kernel(
    core_ref, keys_hbm, value_hbm, decay_hbm, tab_ref, across_ref, send_ref, keys_ref, value_ref, decay_ref, sems
):
    core = core_ref[0]
    copies = [pltpu.make_async_copy(decay_hbm, decay_ref, sems.at[0])]
    for role in (1, 0):
        at = pl.ds(pl.multiple_of((core if role == 0 else 1 - core) * WIDE, WIDE), WIDE)
        for source, target in ((keys_hbm, keys_ref), (value_hbm, value_ref)):
            copies.append(pltpu.make_async_copy(source.at[:, at], target.at[:, at], sems.at[len(copies)]))
    for copy in copies:
        copy.start()
    copies[0].wait()
    down, across = tables(core, decay_ref[...])
    last = down[GROUP - 1 :, :]
    blank = jnp.zeros((GROUP, 128 - 48), F32)
    tab = jnp.concatenate([down, jnp.exp(down), jnp.exp(last - down), blank], axis=1)
    tab_ref[...] = tab
    across_ref[...] = across
    send_ref[WIDE:, :] = jnp.broadcast_to(tab[GROUP - 1 :, :], (8, 128))
    copies[1].wait()
    copies[2].wait()
    for i in range(HALF):
        send_ref[i * DH : (i + 1) * DH, :] = state_term(core, 1, i, keys_ref, value_ref, tab)
    copies[3].wait()
    copies[4].wait()


def second_kernel(core_ref, keys_ref, value_ref, tab_ref, keep_ref):
    core = core_ref[0]
    tab = tab_ref[...]
    for i in range(HALF):
        keep_ref[i * DH : (i + 1) * DH, :] = state_term(core, 0, i, keys_ref, value_ref, tab)


def merge_forward(core_ref, own_ref, other_ref, tab_ref, out_ref, dec_ref):
    zero = core_ref[0] == 0
    mine = tab_ref[GROUP - 1 :, :HALF]
    theirs = other_ref[WIDE : WIDE + 1, HALF : 2 * HALF]
    last_a = jnp.where(zero, mine, theirs)
    last_b = jnp.where(zero, theirs, mine)
    for i in range(HALF):
        own = own_ref[i * DH : (i + 1) * DH, :]
        other = other_ref[i * DH : (i + 1) * DH, :]
        a, b = jnp.where(zero, own, other), jnp.where(zero, other, own)
        here_a = jnp.broadcast_to(last_a[:, i : i + 1], (1, 128))
        here_b = jnp.broadcast_to(last_b[:, i : i + 1], (1, 128))
        dec_ref[i : i + 1, :] = jnp.exp(here_a)
        dec_ref[HALF + i : HALF + i + 1, :] = jnp.exp(here_b)
        out_ref[i, :DH, :] = jnp.exp(here_b) * a + b
        out_ref[i, DH:, :] = jnp.broadcast_to(here_a + here_b, (8, 128))


def merge_backward(core_ref, own_ref, other_ref, dec_ref, out_ref):
    zero = core_ref[0] == 0
    for i in range(HALF):
        own = own_ref[i * DH : (i + 1) * DH, :]
        other = other_ref[i * DH : (i + 1) * DH, :]
        a, b = jnp.where(zero, own, other), jnp.where(zero, other, own)
        out_ref[i] = a + dec_ref[i : i + 1, :] * b


def total_kernel(reverse, parts_ref, decays_ref, out_ref):
    order = list(range(8))[:: -1 if reverse else 1]
    total = parts_ref[order[0], :DH, :]
    for at in order[1:]:
        total = jnp.exp(decays_ref[at, DH : DH + 1, :]) * total + parts_ref[at, :DH, :]
    out_ref[:DH, :] = total
    decay = decays_ref[0, DH:, :]
    for at in range(1, 8):
        decay = decay + decays_ref[at, DH:, :]
    out_ref[DH:, :] = decay


def pair_kernel(reverse, place_ref, own_ref, near_ref, out_ref):
    place = 3 - place_ref[0] if reverse else place_ref[0]
    even = (place == 0) | (place == 2)
    own, near = own_ref[...], near_ref[...]
    first, second = jnp.where(even, own, near), jnp.where(even, near, own)
    out_ref[...] = jnp.exp(second[DH : DH + 1, :]) * first[:DH, :] + second[:DH, :]


def enter_kernel(reverse, place_ref, parts_ref, decays_ref, near_ref, far_ref, out_ref):
    place = 3 - place_ref[0] if reverse else place_ref[0]
    near = jnp.where((place == 1) | (place == 3), near_ref[...], 0.0)
    state = jnp.where(place >= 2, far_ref[...], 0.0)
    state = jnp.exp(near[DH : DH + 1, :]) * state + near[:DH, :]
    order = list(range(8))[:: -1 if reverse else 1]
    for at in order:
        out_ref[at] = state
        if at != order[-1]:
            state = jnp.exp(decays_ref[at, DH : DH + 1, :]) * state + parts_ref[at, :DH, :]


def leave_kernel(reverse, core_ref, enter_ref, own_ref, other_ref, dec_ref, keep_ref, send_ref):
    first = core_ref[0] == (1 if reverse else 0)
    base = HALF if reverse else 0
    for i in range(HALF):
        own = own_ref[i * DH : (i + 1) * DH, :]
        other = other_ref[i * DH : (i + 1) * DH, :]
        nearer = jnp.where(first, own, other)
        x = enter_ref[i]
        y = dec_ref[base + i : base + i + 1, :] * x + nearer
        keep_ref[i] = jnp.where(first, x, y)
        send_ref[i] = jnp.where(first, y, x)


LOW, HIGH = slice(0, DH), slice(DH, GROUP)


def causal(first, middle, last, upper=False):
    blank = jnp.zeros_like(first)
    top, bottom = ([first, middle], [blank, last]) if upper else ([first, blank], [middle, last])
    return jnp.concatenate([jnp.concatenate(top, axis=1), jnp.concatenate(bottom, axis=1)], axis=0)


def masked(array, weights, upper=False):
    middle = array[LOW, HIGH] if upper else array[HIGH, LOW]
    parts = (array[LOW, LOW], middle, array[HIGH, HIGH])
    return causal(*((part * weights[at]).astype(BF16) for at, part in enumerate(parts)), upper=upper)


def intra_kernel(
    role, core_ref, query_ref, keys_ref, value_ref, gate_ref, gain_ref, mixed_ref, tab_ref, across_ref,
    intra_ref, normed_ref, turned_ref, weights_ref,
):
    core = core_ref[0]
    tab = tab_ref[...]
    rows = lax.broadcasted_iota(jnp.int32, (DH, DH), 0)
    cols = lax.broadcasted_iota(jnp.int32, (DH, DH), 1)
    lower, upper = rows >= cols, rows <= cols
    for i in range(HALF):
        at = columns(role, core, i)
        to = slice(i * DH, (i + 1) * DH)
        query, keys = query_ref[:, at], keys_ref[:, at]
        down = lanes(tab, 0, role, i)
        across = across_ref[role * HALF + i : role * HALF + i + 1, :]
        weights = (
            jnp.exp(jnp.where(lower, down[LOW] - across[:, LOW], -jnp.inf)),
            jnp.exp(down[HIGH] - across[:, LOW]),
            jnp.exp(jnp.where(lower, down[HIGH] - across[:, HIGH], -jnp.inf)),
            jnp.exp(jnp.where(upper, across[:, LOW] - down[LOW], -jnp.inf)),
            jnp.exp(across[:, HIGH] - down[LOW]),
            jnp.exp(jnp.where(upper, across[:, HIGH] - down[HIGH], -jnp.inf)),
        )
        for part, array in enumerate(weights):
            weights_ref[i, part] = array
        probs = masked(dot(query, keys, 1, 1), weights[:3])
        turned_ref[i] = masked(dot(keys, query, 1, 1), weights[3:], upper=True)
        intra_ref[:, to] = dot(probs, value_ref[:, at], 1, 0)
        opening = jax.nn.sigmoid(gate_ref[:, at].astype(F32))
        normed_ref[:, to] = mixed_ref[:, at].astype(F32) * opening * gain_ref[:, at]


def attend_kernel(role, core_ref, query_ref, state_ref, intra_ref, normed_ref, tab_ref, *refs):
    if role == 0:
        out_ref, squares_ref, products_ref = refs
        squares, products = jnp.zeros((GROUP, DH), F32), jnp.zeros((GROUP, DH), F32)
    else:
        squares_in, products_in, out_ref, sums_ref = refs
        squares, products = squares_in[...], products_in[...]
    core = core_ref[0]
    tab = tab_ref[...]
    for i in range(HALF):
        at = columns(role, core, i)
        to = slice(i * DH, (i + 1) * DH)
        inter = dot(query_ref[:, at], state_ref[i].astype(BF16), 1, 0)
        attention = intra_ref[:, to] + inter * lanes(tab, 1, role, i)
        out_ref[:, to] = attention
        squares = squares + attention * attention
        products = products + normed_ref[:, to] * attention
    if role == 0:
        squares_ref[...] = squares
        products_ref[...] = products
    else:
        both = [jnp.sum(array.T, axis=0, keepdims=True) for array in (squares, products)]
        sums_ref[...] = jnp.concatenate(both + [jnp.zeros((6, GROUP), F32)], axis=0)


def norm_terms(sums, terms_ref):
    scale = lax.rsqrt(sums[0:1, :] / FEATURES + EPSILON)
    projection = scale * sums[1:2, :] / FEATURES
    both = jnp.concatenate([scale, scale * projection, jnp.zeros((6, GROUP), F32)], axis=0)
    terms_ref[...] = jnp.concatenate([both.T, jnp.zeros((GROUP, DH - 8), F32)], axis=1)


def grad_kernel(role, core_ref, query_ref, attention_ref, normed_ref, tab_ref, terms_ref, grad_ref, term_ref):
    core = core_ref[0]
    tab = tab_ref[...]
    scale, shift = terms_ref[:, 0:1], terms_ref[:, 1:2]
    for i in range(HALF):
        at = columns(role, core, i)
        to = slice(i * DH, (i + 1) * DH)
        grad = (scale * (normed_ref[:, to] - attention_ref[:, to] * shift)).astype(BF16)
        grad_ref[:, to] = grad
        weighted = (query_ref[:, at].astype(F32) * lanes(tab, 1, role, i)).astype(BF16)
        term_ref[i * DH : (i + 1) * DH, :] = dot(turned(weighted), grad, 1, 0)


def grad_first(
    core_ref, query_ref, attention_ref, normed_ref, tab_ref, sum_a, sum_b, sum_c, sum_d, grad_ref, term_ref, terms_ref
):
    norm_terms((sum_a[...] + sum_b[...]) + (sum_c[...] + sum_d[...]), terms_ref)
    grad_kernel(1, core_ref, query_ref, attention_ref, normed_ref, tab_ref, terms_ref, grad_ref, term_ref)


class Sender:
    def __init__(self, role, core, sems):
        self.side = core if role == 0 else 1 - core
        self.sems = sems
        self.copies = []

    def send(self, buf, out, start, width):
        away = pl.ds(pl.multiple_of(self.side * WIDE + start, width), width)
        copy = pltpu.make_async_copy(
            buf.at[:, start : start + width], out.at[:, away], self.sems.at[len(self.copies)]
        )
        copy.start()
        self.copies.append(copy)

    def wait(self):
        for copy in self.copies:
            copy.wait()


def inner_part(
    role, core, query_ref, keys_ref, value_ref, state_ref, grad_ref, turned_ref, weights_ref, tab, keys_out, value_out,
    query_buf, sender, query_out,
):
    for i in range(HALF):
        at = columns(role, core, i)
        to = slice(i * DH, (i + 1) * DH)
        query, keys, value, grad = query_ref[:, at], keys_ref[:, at], value_ref[:, at], grad_ref[:, to]
        weights = [weights_ref[i, part] for part in range(6)]
        scores = masked(dot(grad, value, 1, 1), weights[:3])
        flipped_scores = masked(dot(value, grad, 1, 1), weights[3:], upper=True)
        grad_query = dot(scores, keys, 1, 0)
        grad_query = grad_query + dot(grad, state_ref[i].astype(BF16), 1, 1) * lanes(tab, 1, role, i)
        query_buf[:, to] = grad_query.astype(BF16)
        keys_out[:, to] = dot(flipped_scores, query, 1, 0)
        value_out[:, to] = dot(turned_ref[i], grad, 1, 0)
        if i % 2 == 1:
            sender.send(query_buf, query_out, (i - 1) * DH, 2 * DH)


def local_kernel(
    role, core_ref, query_ref, keys_ref, value_ref, state_ref, grad_ref, turned_ref, weights_ref, tab_ref, mixed_ref,
    gate_ref, terms_ref, *refs
):
    query_out, mixed_out, gate_out, keys_out, value_out, query_buf, mixed_buf, gate_buf, sems = refs[-9:]
    core = core_ref[0]
    tab = tab_ref[...]
    scale = terms_ref[:, 0:1]
    sender = Sender(role, core, sems)
    for i in range(HALF):
        to = slice(i * DH, (i + 1) * DH)
        into = slice(role * WIDE + i * DH, role * WIDE + (i + 1) * DH)
        mixed_buf[:, to] = (mixed_ref[:, into] * scale).astype(BF16)
        gate_buf[:, to] = (gate_ref[:, into] * scale).astype(BF16)
        if i % 4 == 3:
            sender.send(mixed_buf, mixed_out, (i - 3) * DH, 4 * DH)
            sender.send(gate_buf, gate_out, (i - 3) * DH, 4 * DH)
    inner_part(
        role, core, query_ref, keys_ref, value_ref, state_ref, grad_ref, turned_ref, weights_ref, tab, keys_out, value_out,
        query_buf, sender, query_out,
    )
    sender.wait()


def opened_kernel(
    core_ref, gate_ref, gain_ref, upstream_ref, own_ref, other_ref, own_normed, other_normed, mixed_ref, gate_out
):
    core = core_ref[0]
    for role, ref, normed_ref in ((0, own_ref, own_normed), (1, other_ref, other_normed)):
        for i in range(HALF):
            at = columns(role, core, i)
            to = slice(i * DH, (i + 1) * DH)
            into = slice(role * WIDE + i * DH, role * WIDE + (i + 1) * DH)
            opening = jax.nn.sigmoid(gate_ref[:, at].astype(F32))
            attention = ref[:, to]
            mixed_ref[:, into] = attention * (gain_ref[:, at] * opening)
            gate_out[:, into] = normed_ref[:, to] * (attention * (1.0 - opening))


def last_kernel(
    role, core_ref, keys_ref, value_ref, state_ref, part_keys, part_value, tab_ref, *refs
):
    keys_out, value_out, keys_buf, value_buf, sems = refs[-5:]
    core = core_ref[0]
    tab = tab_ref[...]
    sender = Sender(role, core, sems)
    for i in range(HALF):
        at = columns(role, core, i)
        to = slice(i * DH, (i + 1) * DH)
        state = state_ref[i].astype(BF16)
        toward_end = lanes(tab, 2, role, i)
        grad_keys = part_keys[:, to] + dot(value_ref[:, at], state, 1, 1) * toward_end
        grad_value = part_value[:, to] + dot(keys_ref[:, at], state, 1, 0) * toward_end
        keys_buf[:, to] = grad_keys.astype(BF16)
        value_buf[:, to] = grad_value.astype(BF16)
        if i % 2 == 1:
            for buf, out in ((keys_buf, keys_out), (value_buf, value_out)):
                sender.send(buf, out, (i - 1) * DH, 2 * DH)
    sender.wait()


def swap(array):
    return lax.ppermute(array, "core", [(0, 1), (1, 0)])


def flipped(array, axis, flip):
    return lax.ppermute(array, axis, [(i, i ^ flip) for i in range(4)])


def spread(array):
    return lax.all_to_all(array, PLANE, 0, 0, tiled=True)


def scan(core, place, own, other, tab, dec, decays, reverse, beside):
    if reverse:
        totals = call(merge_backward, shape(HALF, DH, DH), core, own, other, dec, name="merge_b")
    else:
        totals, dec = call(
            merge_forward, (shape(HALF, DH + 8, DH), shape(2 * HALF, DH)), core, own, other, tab, name="merge_f"
        )
    parts = spread(totals)
    decays = parts if decays is None else decays
    row = call(
        functools.partial(total_kernel, reverse), shape(DH + 8, DH), parts, decays, smem=0, name="row_total"
    )
    near, done = lax.optimization_barrier((flipped(row, "z1", 1), beside(row, 0, ())))
    pair = call(functools.partial(pair_kernel, reverse), shape(DH, DH), place, row, near, name="pair")
    far, done = lax.optimization_barrier((flipped(pair, "z1", 3), beside(pair, 1, done)))
    entering = call(
        functools.partial(enter_kernel, reverse), shape(8, DH, DH), place, parts, decays, near, far, name="enter"
    )
    entering = spread(entering)
    keep, send = call(
        functools.partial(leave_kernel, reverse),
        (shape(HALF, DH, DH), shape(HALF, DH, DH)),
        core, entering, own, other, dec, name="leave",
    )
    return keep, swap(send), dec, decays, done


def on_device(query, keys, value, gate, decay, gain, upstream):
    core, place = lax.optimization_barrier(
        [lax.axis_index(axis).astype(jnp.int32).reshape(1) for axis in ("core", "z1")]
    )
    gain = gain.reshape(1, -1)
    big = 2 * GROUP * GROUP * DH * HALF
    small = big // 2

    full = shape(GROUP, 2 * WIDE, dtype=BF16)
    tab, across, send, keys, value = call(
        first_kernel,
        (shape(GROUP, 128), shape(16, GROUP), shape(WIDE + 8, DH), full, full),
        core, *(pltpu.with_memory_space_constraint(a, pltpu.HBM) for a in (keys, value, decay.T)),
        flops=small, name="first",
        specs=[SMEM, HBM, HBM, HBM], scratch=[pltpu.VMEM((16, GROUP), F32), pltpu.SemaphoreType.DMA((5,))],
    )
    other = swap(send)
    own = call(second_kernel, shape(WIDE, DH), core, keys, value, tab, flops=small, name="second")

    wide = shape(GROUP, WIDE)
    probs_shape = shape(HALF, GROUP, GROUP, dtype=BF16)
    weights_shape = shape(HALF, 6, DH, DH)

    def intra_part(after, role, done):
        held, _ = lax.optimization_barrier((query, after))
        results = call(
            functools.partial(intra_kernel, role), (wide, wide, probs_shape, weights_shape),
            core, held, keys, value, gate, gain, upstream, tab, across, flops=3 * big, name=f"intra{role}",
        )
        return (*done, results)

    state_own, state_other, dec, decays, intra = scan(
        core, place, own, other, tab, None, None, False, intra_part
    )

    narrow = shape(GROUP, DH)
    att_own, *partial = call(
        functools.partial(attend_kernel, 0), (wide, narrow, narrow),
        core, query, state_own, *intra[0][:2], tab, flops=small, name="attend0",
    )
    att_other, sums = call(
        functools.partial(attend_kernel, 1), (wide, shape(8, GROUP)),
        core, query, state_other, *intra[1][:2], tab, *partial, flops=small, name="attend1",
    )
    opened = call(
        opened_kernel, (shape(GROUP, 2 * WIDE), shape(GROUP, 2 * WIDE)),
        core, gate, gain, upstream, att_own, att_other, intra[0][1], intra[1][1], name="opened",
    )
    moved = [flipped(sums, "head", flip) for flip in (1, 2, 3)]
    moved, opened = lax.optimization_barrier((moved, opened))

    grads_shape = (shape(GROUP, WIDE, dtype=BF16), shape(WIDE, DH))
    grad_other, term_send, terms = call(
        grad_first, (*grads_shape, shape(GROUP, DH)),
        core, query, att_other, intra[1][1], tab, sums, *moved, flops=small, name="grad1",
    )
    term_other = swap(term_send)
    grad_own, term_own = call(
        functools.partial(grad_kernel, 0), grads_shape, core, query, att_own, intra[0][1], tab, terms,
        flops=small, name="grad0",
    )

    half = pltpu.VMEM((GROUP, WIDE), BF16)

    whole = pltpu.HBM((GROUP, 2 * WIDE), BF16)

    def local(after, role, done):
        held, factors, _ = lax.optimization_barrier((query, terms, after))
        state, grad = ((state_own, grad_own), (state_other, grad_other))[role]
        sent = done[:3]
        results = call(
            functools.partial(local_kernel, role), (whole, whole, whole, wide, wide),
            core, held, keys, value, state, grad, *intra[role][2:], tab, *opened, factors, *sent,
            flops=5 * big, name=f"local{role}", limit=10,
            specs=[SMEM] + [VMEM] * 11 + [HBM] * len(sent), outs=(HBM, HBM, HBM, VMEM, VMEM),
            scratch=[half] * 3 + [pltpu.SemaphoreType.DMA((8,))],
            aliases={12: 0, 13: 1, 14: 2} if sent else None,
        )
        return (*results[:3], *done[3:], *results[3:])

    after_own, after_other, _, _, (grad_query, mixed, grad_gate, *inner) = scan(
        core, place, term_own, term_other, tab, dec, decays, True, local
    )
    ends = ()
    for role, state in ((0, after_own), (1, after_other)):
        ends = call(
            functools.partial(last_kernel, role), (full, full),
            core, keys, value, state, *inner[2 * role : 2 * role + 2], tab, *ends, flops=2 * small, name=f"last{role}",
            specs=[SMEM] + [VMEM] * 6 + [HBM] * len(ends), outs=(HBM, HBM),
            scratch=[half, half, pltpu.SemaphoreType.DMA((8,))], aliases={7: 0, 8: 1} if ends else None,
        )
    grad_keys, grad_value = ends
    return mixed, grad_query, grad_keys, grad_value, grad_gate


def solution(mesh):
    levels = Mesh(mesh.devices.reshape(4, 2, 4, 2, 4), ("z1", "z0", "y", "core", "head"))
    seq = ("z1", "z0", "y", "core")
    both = P(seq, "head")
    return jax.shard_map(
        on_device,
        mesh=levels,
        in_specs=(both, both, both, both, both, P("head"), both),
        out_specs=(both,) * 5,
        check_vma=False,
    )
```

```python
import functools
import math

import jax
import jax.numpy as jnp
from jax import lax
from jax.experimental import pallas as pl
from jax.experimental.pallas import tpu as pltpu
from jax.sharding import Mesh, PartitionSpec as P

DH = 128
GROUP = 256
HALF = 8
WIDE = HALF * DH
FEATURES = 64 * DH
EPSILON = 1e-06
F32 = jnp.float32
BF16 = jnp.bfloat16
PLANE = ("z0", "y")
VMEM = pl.BlockSpec(memory_space=pltpu.VMEM)
SMEM = pl.BlockSpec(memory_space=pltpu.SMEM)
HBM = pl.BlockSpec(memory_space=pltpu.HBM)


def call(kernel, out, *args, flops=0, smem=1, limit=6, name=None, specs=None, outs=None, scratch=(), aliases=None):
    moved = sum(a.size * a.dtype.itemsize for a in args)
    moved += sum(math.prod(o.shape) * 4 for o in jax.tree.leaves(out))
    return pl.pallas_call(
        kernel,
        out_shape=out,
        in_specs=specs or [SMEM] * smem + [VMEM] * (len(args) - smem),
        out_specs=outs or jax.tree.map(lambda _: VMEM, out),
        scratch_shapes=scratch,
        input_output_aliases=aliases or {},
        compiler_params=pltpu.CompilerParams(vmem_limit_bytes=limit << 20),
        cost_estimate=pl.CostEstimate(flops=flops, bytes_accessed=moved, transcendentals=0),
        name=name,
    )(*args)


def shape(*dims, dtype=F32):
    return jax.ShapeDtypeStruct(dims, dtype)


def dot(a, b, ca, cb, precision=None):
    return lax.dot_general(
        a, b, (((ca,), (cb,)), ((), ())), precision=precision, preferred_element_type=F32
    )


def turned(x):
    rows = lax.broadcasted_iota(jnp.int32, (DH, DH), 0)
    cols = lax.broadcasted_iota(jnp.int32, (DH, DH), 1)
    return dot((rows == cols).astype(BF16), x, 1, 1)


def columns(role, core, i):
    side = core if role == 0 else 1 - core
    return pl.ds(pl.multiple_of(side * WIDE + i * DH, DH), DH)


def lanes(tab, which, role, i):
    at = which * 16 + role * HALF + i
    return tab[:, at : at + 1]


def tables(core, decays):
    rows = lax.broadcasted_iota(jnp.int32, (GROUP, GROUP), 0)
    cols = lax.broadcasted_iota(jnp.int32, (GROUP, GROUP), 1)
    tri = (rows >= cols).astype(BF16)
    high = decays.astype(BF16)
    rest = decays - high.astype(F32)
    middle = rest.astype(BF16)
    low = (rest - middle.astype(F32)).astype(BF16)
    across = dot(jnp.concatenate([high, middle, low], axis=0), tri, 1, 1)
    across = across[:16] + (across[16:32] + across[32:])
    return jnp.where(core == 0, across, jnp.concatenate([across[HALF:], across[:HALF]], axis=0))


def state_term(core, role, i, keys_ref, value_ref, toward_end):
    at = columns(role, core, i)
    row = toward_end[role * HALF + i : role * HALF + i + 1, :]
    keyed = (turned(keys_ref[:, at]) * row).astype(BF16)
    return dot(keyed, value_ref[:, at], 1, 0)


def toward_last(across):
    return jnp.exp(across[:, GROUP - 1 :] - across)


def first_kernel(
    core_ref, keys_hbm, value_hbm, decay_hbm, across_ref, send_ref, keys_ref, value_ref, decay_ref, sems
):
    core = core_ref[0]
    copies = [pltpu.make_async_copy(decay_hbm, decay_ref, sems.at[0])]
    for role in (1, 0):
        at = pl.ds(pl.multiple_of((core if role == 0 else 1 - core) * WIDE, WIDE), WIDE)
        for source, target in ((keys_hbm, keys_ref), (value_hbm, value_ref)):
            copies.append(pltpu.make_async_copy(source.at[:, at], target.at[:, at], sems.at[len(copies)]))
    for copy in copies:
        copy.start()
    copies[0].wait()
    across = tables(core, decay_ref[...])
    across_ref[...] = across
    send_ref[WIDE:, :] = jnp.broadcast_to(across[:, GROUP - 1 :], (16, DH))
    toward_end = toward_last(across)
    copies[1].wait()
    copies[2].wait()
    for i in range(HALF):
        send_ref[i * DH : (i + 1) * DH, :] = state_term(core, 1, i, keys_ref, value_ref, toward_end)
    copies[3].wait()
    copies[4].wait()


def second_kernel(core_ref, keys_ref, value_ref, across_ref, tab_ref, keep_ref):
    core = core_ref[0]
    across = across_ref[...]
    down = across.T
    last = down[GROUP - 1 :, :]
    blank = jnp.zeros((GROUP, 128 - 48), F32)
    tab_ref[...] = jnp.concatenate([down, jnp.exp(down), jnp.exp(last - down), blank], axis=1)
    toward_end = toward_last(across)
    for i in range(HALF):
        keep_ref[i * DH : (i + 1) * DH, :] = state_term(core, 0, i, keys_ref, value_ref, toward_end)


def merge_forward(core_ref, own_ref, other_ref, across_ref, out_ref, dec_ref):
    zero = core_ref[0] == 0
    mine = jnp.broadcast_to(across_ref[:HALF, GROUP - 1 :], (HALF, DH))
    theirs = other_ref[WIDE + HALF :, :]
    decay = mine + theirs
    factor = jnp.exp(jnp.where(zero, theirs, mine))
    dec_ref[:HALF, :] = jnp.exp(jnp.where(zero, mine, theirs))
    dec_ref[HALF:, :] = factor
    own_factor, other_factor = jnp.where(zero, factor, 1.0), jnp.where(zero, 1.0, factor)
    for i in range(HALF):
        at = slice(i * DH, (i + 1) * DH)
        out_ref[i, :DH, :] = own_factor[i : i + 1] * own_ref[at, :] + other_factor[i : i + 1] * other_ref[at, :]
        out_ref[i, DH:, :] = jnp.broadcast_to(decay[i : i + 1], (8, DH))


def merge_backward(core_ref, own_ref, other_ref, dec_ref, out_ref):
    zero = core_ref[0] == 0
    for i in range(HALF):
        own = own_ref[i * DH : (i + 1) * DH, :]
        other = other_ref[i * DH : (i + 1) * DH, :]
        a, b = jnp.where(zero, own, other), jnp.where(zero, other, own)
        out_ref[i] = a + dec_ref[i : i + 1, :] * b


def total_kernel(reverse, parts_ref, decays_ref, out_ref):
    order = list(range(8))[:: -1 if reverse else 1]
    total = parts_ref[order[0], :DH, :]
    for at in order[1:]:
        total = jnp.exp(decays_ref[at, DH : DH + 1, :]) * total + parts_ref[at, :DH, :]
    out_ref[:DH, :] = total
    decay = decays_ref[0, DH:, :]
    for at in range(1, 8):
        decay = decay + decays_ref[at, DH:, :]
    out_ref[DH:, :] = decay


def pair_kernel(reverse, place_ref, own_ref, near_ref, out_ref):
    place = 3 - place_ref[0] if reverse else place_ref[0]
    even = (place == 0) | (place == 2)
    own, near = own_ref[...], near_ref[...]
    first, second = jnp.where(even, own, near), jnp.where(even, near, own)
    out_ref[...] = jnp.exp(second[DH : DH + 1, :]) * first[:DH, :] + second[:DH, :]


def enter_kernel(reverse, place_ref, parts_ref, decays_ref, near_ref, far_ref, out_ref):
    place = 3 - place_ref[0] if reverse else place_ref[0]
    near = jnp.where((place == 1) | (place == 3), near_ref[...], 0.0)
    state = jnp.where(place >= 2, far_ref[...], 0.0)
    state = jnp.exp(near[DH : DH + 1, :]) * state + near[:DH, :]
    order = list(range(8))[:: -1 if reverse else 1]
    for at in order:
        out_ref[at] = state
        if at != order[-1]:
            state = jnp.exp(decays_ref[at, DH : DH + 1, :]) * state + parts_ref[at, :DH, :]


def leave_kernel(reverse, core_ref, enter_ref, own_ref, other_ref, dec_ref, keep_ref, send_ref):
    first = core_ref[0] == (1 if reverse else 0)
    base = HALF if reverse else 0
    for i in range(HALF):
        own = own_ref[i * DH : (i + 1) * DH, :]
        other = other_ref[i * DH : (i + 1) * DH, :]
        nearer = jnp.where(first, own, other)
        x = enter_ref[i]
        y = dec_ref[base + i : base + i + 1, :] * x + nearer
        keep_ref[i] = jnp.where(first, x, y)
        send_ref[i] = jnp.where(first, y, x)


LOW, HIGH = slice(0, DH), slice(DH, GROUP)


def causal(first, middle, last, upper=False):
    blank = jnp.zeros_like(first)
    top, bottom = ([first, middle], [blank, last]) if upper else ([first, blank], [middle, last])
    return jnp.concatenate([jnp.concatenate(top, axis=1), jnp.concatenate(bottom, axis=1)], axis=0)


def masked(array, weights, upper=False):
    middle = array[LOW, HIGH] if upper else array[HIGH, LOW]
    parts = (array[LOW, LOW], middle, array[HIGH, HIGH])
    return causal(*((part * weights[at]).astype(BF16) for at, part in enumerate(parts)), upper=upper)


def intra_kernel(
    role, core_ref, query_ref, keys_ref, value_ref, gate_ref, gain_ref, mixed_ref, tab_ref, across_ref,
    intra_ref, normed_ref, turned_ref, weights_ref, weighted_ref,
):
    core = core_ref[0]
    tab = tab_ref[...]
    rows = lax.broadcasted_iota(jnp.int32, (DH, DH), 0)
    cols = lax.broadcasted_iota(jnp.int32, (DH, DH), 1)
    lower, upper = rows >= cols, rows <= cols
    for i in range(HALF):
        at = columns(role, core, i)
        to = slice(i * DH, (i + 1) * DH)
        query, keys = query_ref[:, at], keys_ref[:, at]
        down = lanes(tab, 0, role, i)
        across = across_ref[role * HALF + i : role * HALF + i + 1, :]
        weights = (
            jnp.exp(jnp.where(lower, down[LOW] - across[:, LOW], -jnp.inf)),
            jnp.exp(down[HIGH] - across[:, LOW]),
            jnp.exp(jnp.where(lower, down[HIGH] - across[:, HIGH], -jnp.inf)),
            jnp.exp(jnp.where(upper, across[:, LOW] - down[LOW], -jnp.inf)),
            jnp.exp(across[:, HIGH] - down[LOW]),
            jnp.exp(jnp.where(upper, across[:, HIGH] - down[HIGH], -jnp.inf)),
        )
        for part, array in enumerate(weights):
            weights_ref[i, part] = array
        weighted_ref[i] = (turned(query) * jnp.exp(across)).astype(BF16)
        probs = masked(dot(query, keys, 1, 1), weights[:3])
        turned_ref[i] = masked(dot(keys, query, 1, 1), weights[3:], upper=True)
        intra_ref[:, to] = dot(probs, value_ref[:, at], 1, 0)
        opening = jax.nn.sigmoid(gate_ref[:, at].astype(F32))
        normed_ref[:, to] = mixed_ref[:, at].astype(F32) * opening * gain_ref[:, at]


def attend_kernel(role, core_ref, query_ref, state_ref, intra_ref, normed_ref, tab_ref, *refs):
    if role == 0:
        out_ref, squares_ref, products_ref = refs
        squares, products = jnp.zeros((GROUP, DH), F32), jnp.zeros((GROUP, DH), F32)
    else:
        squares_in, products_in, out_ref, sums_ref = refs
        squares, products = squares_in[...], products_in[...]
    core = core_ref[0]
    tab = tab_ref[...]
    for i in range(HALF):
        at = columns(role, core, i)
        to = slice(i * DH, (i + 1) * DH)
        inter = dot(query_ref[:, at], state_ref[i].astype(BF16), 1, 0)
        attention = intra_ref[:, to] + inter * lanes(tab, 1, role, i)
        out_ref[:, to] = attention
        squares = squares + attention * attention
        products = products + normed_ref[:, to] * attention
    if role == 0:
        squares_ref[...] = squares
        products_ref[...] = products
    else:
        both = [jnp.sum(array.T, axis=0, keepdims=True) for array in (squares, products)]
        sums_ref[...] = jnp.concatenate(both + [jnp.zeros((6, GROUP), F32)], axis=0)


def norm_terms(sums, terms_ref):
    scale = lax.rsqrt(sums[0:1, :] / FEATURES + EPSILON)
    projection = scale * sums[1:2, :] / FEATURES
    both = jnp.concatenate([scale, scale * projection, jnp.zeros((6, GROUP), F32)], axis=0)
    terms_ref[...] = jnp.concatenate([both.T, jnp.zeros((GROUP, DH - 8), F32)], axis=1)


def grad_kernel(attention_ref, normed_ref, weighted_ref, terms_ref, grad_ref, term_ref):
    scale, shift = terms_ref[:, 0:1], terms_ref[:, 1:2]
    for i in range(HALF):
        to = slice(i * DH, (i + 1) * DH)
        grad = (scale * (normed_ref[:, to] - attention_ref[:, to] * shift)).astype(BF16)
        grad_ref[:, to] = grad
        term_ref[i * DH : (i + 1) * DH, :] = dot(weighted_ref[i], grad, 1, 0)


def grad_first(
    attention_ref, normed_ref, weighted_ref, sum_a, sum_b, sum_c, sum_d, grad_ref, term_ref, terms_ref
):
    norm_terms((sum_a[...] + sum_b[...]) + (sum_c[...] + sum_d[...]), terms_ref)
    grad_kernel(attention_ref, normed_ref, weighted_ref, terms_ref, grad_ref, term_ref)


class Sender:
    def __init__(self, role, core, sems):
        self.side = core if role == 0 else 1 - core
        self.sems = sems
        self.copies = []

    def send(self, buf, out, start, width):
        away = pl.ds(pl.multiple_of(self.side * WIDE + start, width), width)
        copy = pltpu.make_async_copy(
            buf.at[:, start : start + width], out.at[:, away], self.sems.at[len(self.copies)]
        )
        copy.start()
        self.copies.append(copy)

    def wait(self):
        for copy in self.copies:
            copy.wait()


def inner_part(
    role, core, query_ref, keys_ref, value_ref, state_ref, grad_ref, turned_ref, weights_ref, tab, keys_out, value_out,
    query_buf, sender, query_out,
):
    for i in range(HALF):
        at = columns(role, core, i)
        to = slice(i * DH, (i + 1) * DH)
        query, keys, value, grad = query_ref[:, at], keys_ref[:, at], value_ref[:, at], grad_ref[:, to]
        weights = [weights_ref[i, part] for part in range(6)]
        scores = masked(dot(grad, value, 1, 1), weights[:3])
        flipped_scores = masked(dot(value, grad, 1, 1), weights[3:], upper=True)
        grad_query = dot(scores, keys, 1, 0)
        grad_query = grad_query + dot(grad, state_ref[i].astype(BF16), 1, 1) * lanes(tab, 1, role, i)
        query_buf[:, to] = grad_query.astype(BF16)
        keys_out[:, to] = dot(flipped_scores, query, 1, 0)
        value_out[:, to] = dot(turned_ref[i], grad, 1, 0)
        if i % 2 == 1:
            sender.send(query_buf, query_out, (i - 1) * DH, 2 * DH)


def local_kernel(
    role, core_ref, query_ref, keys_ref, value_ref, state_ref, grad_ref, turned_ref, weights_ref, tab_ref, mixed_ref,
    gate_ref, terms_ref, *refs
):
    query_out, mixed_out, gate_out, keys_out, value_out, query_buf, mixed_buf, gate_buf, sems = refs[-9:]
    core = core_ref[0]
    tab = tab_ref[...]
    scale = terms_ref[:, 0:1]
    sender = Sender(role, core, sems)
    for i in range(HALF):
        to = slice(i * DH, (i + 1) * DH)
        into = slice(role * WIDE + i * DH, role * WIDE + (i + 1) * DH)
        mixed_buf[:, to] = (mixed_ref[:, into] * scale).astype(BF16)
        gate_buf[:, to] = (gate_ref[:, into] * scale).astype(BF16)
        if i % 4 == 3:
            sender.send(mixed_buf, mixed_out, (i - 3) * DH, 4 * DH)
            sender.send(gate_buf, gate_out, (i - 3) * DH, 4 * DH)
    inner_part(
        role, core, query_ref, keys_ref, value_ref, state_ref, grad_ref, turned_ref, weights_ref, tab, keys_out, value_out,
        query_buf, sender, query_out,
    )
    sender.wait()


def opened_kernel(
    core_ref, gate_ref, gain_ref, upstream_ref, own_ref, other_ref, own_normed, other_normed, mixed_ref, gate_out
):
    core = core_ref[0]
    for role, ref, normed_ref in ((0, own_ref, own_normed), (1, other_ref, other_normed)):
        for i in range(HALF):
            at = columns(role, core, i)
            to = slice(i * DH, (i + 1) * DH)
            into = slice(role * WIDE + i * DH, role * WIDE + (i + 1) * DH)
            opening = jax.nn.sigmoid(gate_ref[:, at].astype(F32))
            attention = ref[:, to]
            mixed_ref[:, into] = attention * (gain_ref[:, at] * opening)
            gate_out[:, into] = normed_ref[:, to] * (attention * (1.0 - opening))


def last_kernel(
    role, core_ref, keys_ref, value_ref, state_ref, part_keys, part_value, tab_ref, *refs
):
    keys_out, value_out, keys_buf, value_buf, sems = refs[-5:]
    core = core_ref[0]
    tab = tab_ref[...]
    sender = Sender(role, core, sems)
    for i in range(HALF):
        at = columns(role, core, i)
        to = slice(i * DH, (i + 1) * DH)
        state = state_ref[i].astype(BF16)
        toward_end = lanes(tab, 2, role, i)
        grad_keys = part_keys[:, to] + dot(value_ref[:, at], state, 1, 1) * toward_end
        grad_value = part_value[:, to] + dot(keys_ref[:, at], state, 1, 0) * toward_end
        keys_buf[:, to] = grad_keys.astype(BF16)
        value_buf[:, to] = grad_value.astype(BF16)
        if i % 2 == 1:
            for buf, out in ((keys_buf, keys_out), (value_buf, value_out)):
                sender.send(buf, out, (i - 1) * DH, 2 * DH)
    sender.wait()


def swap(array):
    return lax.ppermute(array, "core", [(0, 1), (1, 0)])


def flipped(array, axis, flip):
    return lax.ppermute(array, axis, [(i, i ^ flip) for i in range(4)])


def spread(array):
    return lax.all_to_all(array, PLANE, 0, 0, tiled=True)


def scan(core, place, own, other, across, dec, decays, reverse, beside):
    if reverse:
        totals = call(merge_backward, shape(HALF, DH, DH), core, own, other, dec, name="merge_b")
    else:
        totals, dec = call(
            merge_forward, (shape(HALF, DH + 8, DH), shape(2 * HALF, DH)), core, own, other, across, name="merge_f"
        )
    parts = spread(totals)
    decays = parts if decays is None else decays
    row = call(
        functools.partial(total_kernel, reverse), shape(DH + 8, DH), parts, decays, smem=0, name="row_total"
    )
    near, done = lax.optimization_barrier((flipped(row, "z1", 1), beside(row, 0, ())))
    pair = call(functools.partial(pair_kernel, reverse), shape(DH, DH), place, row, near, name="pair")
    far, done = lax.optimization_barrier((flipped(pair, "z1", 3), beside(pair, 1, done)))
    entering = call(
        functools.partial(enter_kernel, reverse), shape(8, DH, DH), place, parts, decays, near, far, name="enter"
    )
    entering = spread(entering)
    keep, send = call(
        functools.partial(leave_kernel, reverse),
        (shape(HALF, DH, DH), shape(HALF, DH, DH)),
        core, entering, own, other, dec, name="leave",
    )
    return keep, swap(send), dec, decays, done


def on_device(query, keys, value, gate, decay, gain, upstream):
    core, place = lax.optimization_barrier(
        [lax.axis_index(axis).astype(jnp.int32).reshape(1) for axis in ("core", "z1")]
    )
    gain = gain.reshape(1, -1)
    big = 2 * GROUP * GROUP * DH * HALF
    small = big // 2

    full = shape(GROUP, 2 * WIDE, dtype=BF16)
    across, send, keys, value = call(
        first_kernel,
        (shape(16, GROUP), shape(WIDE + 16, DH), full, full),
        core, *(pltpu.with_memory_space_constraint(a, pltpu.HBM) for a in (keys, value, decay.T)),
        flops=small, name="first",
        specs=[SMEM, HBM, HBM, HBM], scratch=[pltpu.VMEM((16, GROUP), F32), pltpu.SemaphoreType.DMA((5,))],
    )
    other = swap(send)
    tab, own = call(
        second_kernel, (shape(GROUP, 128), shape(WIDE, DH)), core, keys, value, across, flops=small, name="second"
    )

    wide = shape(GROUP, WIDE)
    probs_shape = shape(HALF, GROUP, GROUP, dtype=BF16)
    weights_shape = shape(HALF, 6, DH, DH)
    weighted_shape = shape(HALF, DH, GROUP, dtype=BF16)

    def intra_part(after, role, done):
        held, _ = lax.optimization_barrier((query, after))
        results = call(
            functools.partial(intra_kernel, role), (wide, wide, probs_shape, weights_shape, weighted_shape),
            core, held, keys, value, gate, gain, upstream, tab, across, flops=3 * big, name=f"intra{role}",
        )
        return (*done, results)

    state_own, state_other, dec, decays, intra = scan(
        core, place, own, other, across, None, None, False, intra_part
    )

    narrow = shape(GROUP, DH)
    att_own, *partial = call(
        functools.partial(attend_kernel, 0), (wide, narrow, narrow),
        core, query, state_own, *intra[0][:2], tab, flops=small, name="attend0",
    )
    att_other, sums = call(
        functools.partial(attend_kernel, 1), (wide, shape(8, GROUP)),
        core, query, state_other, *intra[1][:2], tab, *partial, flops=small, name="attend1",
    )
    opened = call(
        opened_kernel, (shape(GROUP, 2 * WIDE), shape(GROUP, 2 * WIDE)),
        core, gate, gain, upstream, att_own, att_other, intra[0][1], intra[1][1], name="opened",
    )
    moved = [flipped(sums, "head", flip) for flip in (1, 2, 3)]
    moved, opened = lax.optimization_barrier((moved, opened))

    grads_shape = (shape(GROUP, WIDE, dtype=BF16), shape(WIDE, DH))
    grad_other, term_send, terms = call(
        grad_first, (*grads_shape, shape(GROUP, DH)),
        att_other, intra[1][1], intra[1][4], sums, *moved, flops=small, smem=0, name="grad1",
    )
    term_other = swap(term_send)
    grad_own, term_own = call(
        grad_kernel, grads_shape, att_own, intra[0][1], intra[0][4], terms, flops=small, smem=0, name="grad0",
    )

    half = pltpu.VMEM((GROUP, WIDE), BF16)

    whole = pltpu.HBM((GROUP, 2 * WIDE), BF16)

    def local(after, role, done):
        held, factors, _ = lax.optimization_barrier((query, terms, after))
        state, grad = ((state_own, grad_own), (state_other, grad_other))[role]
        sent = done[:3]
        results = call(
            functools.partial(local_kernel, role), (whole, whole, whole, wide, wide),
            core, held, keys, value, state, grad, *intra[role][2:4], tab, *opened, factors, *sent,
            flops=5 * big, name=f"local{role}", limit=10,
            specs=[SMEM] + [VMEM] * 11 + [HBM] * len(sent), outs=(HBM, HBM, HBM, VMEM, VMEM),
            scratch=[half] * 3 + [pltpu.SemaphoreType.DMA((8,))],
            aliases={12: 0, 13: 1, 14: 2} if sent else None,
        )
        return (*results[:3], *done[3:], *results[3:])

    after_own, after_other, _, _, (grad_query, mixed, grad_gate, *inner) = scan(
        core, place, term_own, term_other, across, dec, decays, True, local
    )
    ends = ()
    for role, state in ((0, after_own), (1, after_other)):
        ends = call(
            functools.partial(last_kernel, role), (full, full),
            core, keys, value, state, *inner[2 * role : 2 * role + 2], tab, *ends, flops=2 * small, name=f"last{role}",
            specs=[SMEM] + [VMEM] * 6 + [HBM] * len(ends), outs=(HBM, HBM),
            scratch=[half, half, pltpu.SemaphoreType.DMA((8,))], aliases={7: 0, 8: 1} if ends else None,
        )
    grad_keys, grad_value = ends
    return mixed, grad_query, grad_keys, grad_value, grad_gate


def solution(mesh):
    levels = Mesh(mesh.devices.reshape(4, 2, 4, 2, 4), ("z1", "z0", "y", "core", "head"))
    seq = ("z1", "z0", "y", "core")
    both = P(seq, "head")
    return jax.shard_map(
        on_device,
        mesh=levels,
        in_specs=(both, both, both, both, both, P("head"), both),
        out_specs=(both,) * 5,
        check_vma=False,
    )
```

```python
import functools
import math

import jax
import jax.numpy as jnp
from jax import lax
from jax.experimental import pallas as pl
from jax.experimental.pallas import tpu as pltpu
from jax.sharding import Mesh, PartitionSpec as P

DH = 128
GROUP = 256
HALF = 8
WIDE = HALF * DH
FEATURES = 64 * DH
EPSILON = 1e-06
F32 = jnp.float32
BF16 = jnp.bfloat16
PLANE = ("z0", "y")
VMEM = pl.BlockSpec(memory_space=pltpu.VMEM)
SMEM = pl.BlockSpec(memory_space=pltpu.SMEM)
HBM = pl.BlockSpec(memory_space=pltpu.HBM)


def call(kernel, out, *args, flops=0, smem=1, limit=6, name=None, specs=None, outs=None, scratch=(), aliases=None):
    moved = sum(a.size * a.dtype.itemsize for a in args)
    moved += sum(math.prod(o.shape) * 4 for o in jax.tree.leaves(out))
    return pl.pallas_call(
        kernel,
        out_shape=out,
        in_specs=specs or [SMEM] * smem + [VMEM] * (len(args) - smem),
        out_specs=outs or jax.tree.map(lambda _: VMEM, out),
        scratch_shapes=scratch,
        input_output_aliases=aliases or {},
        compiler_params=pltpu.CompilerParams(vmem_limit_bytes=limit << 20),
        cost_estimate=pl.CostEstimate(flops=flops, bytes_accessed=moved, transcendentals=0),
        name=name,
    )(*args)


def shape(*dims, dtype=F32):
    return jax.ShapeDtypeStruct(dims, dtype)


def dot(a, b, ca, cb, precision=None):
    return lax.dot_general(
        a, b, (((ca,), (cb,)), ((), ())), precision=precision, preferred_element_type=F32
    )


def turned(x):
    rows = lax.broadcasted_iota(jnp.int32, (DH, DH), 0)
    cols = lax.broadcasted_iota(jnp.int32, (DH, DH), 1)
    return dot((rows == cols).astype(BF16), x, 1, 1)


def columns(role, core, i):
    side = core if role == 0 else 1 - core
    return pl.ds(pl.multiple_of(side * WIDE + i * DH, DH), DH)


def lanes(tab, which, role, i):
    at = which * 16 + role * HALF + i
    return tab[:, at : at + 1]


def tables(core, decays):
    rows = lax.broadcasted_iota(jnp.int32, (GROUP, GROUP), 0)
    cols = lax.broadcasted_iota(jnp.int32, (GROUP, GROUP), 1)
    tri = (rows >= cols).astype(BF16)
    high = decays.astype(BF16)
    rest = decays - high.astype(F32)
    middle = rest.astype(BF16)
    low = (rest - middle.astype(F32)).astype(BF16)
    across = dot(jnp.concatenate([high, middle, low], axis=0), tri, 1, 1)
    across = across[:16] + (across[16:32] + across[32:])
    return jnp.where(core == 0, across, jnp.concatenate([across[HALF:], across[:HALF]], axis=0))


def state_term(core, role, i, keys_ref, value_ref, toward_end):
    at = columns(role, core, i)
    row = toward_end[role * HALF + i : role * HALF + i + 1, :]
    keyed = (turned(keys_ref[:, at]) * row).astype(BF16)
    return dot(keyed, value_ref[:, at], 1, 0)


def toward_last(across):
    return jnp.exp(across[:, GROUP - 1 :] - across)


def first_kernel(
    core_ref, keys_hbm, value_hbm, decay_hbm, across_ref, send_ref, keys_ref, value_ref, decay_ref, sems
):
    core = core_ref[0]
    copies = [pltpu.make_async_copy(decay_hbm, decay_ref, sems.at[0])]
    for role in (1, 0):
        at = pl.ds(pl.multiple_of((core if role == 0 else 1 - core) * WIDE, WIDE), WIDE)
        for source, target in ((keys_hbm, keys_ref), (value_hbm, value_ref)):
            copies.append(pltpu.make_async_copy(source.at[:, at], target.at[:, at], sems.at[len(copies)]))
    for copy in copies:
        copy.start()
    copies[0].wait()
    across = tables(core, decay_ref[...])
    across_ref[...] = across
    send_ref[WIDE:, :] = jnp.broadcast_to(across[:, GROUP - 1 :], (16, DH))
    toward_end = toward_last(across)
    copies[1].wait()
    copies[2].wait()
    for i in range(HALF):
        send_ref[i * DH : (i + 1) * DH, :] = state_term(core, 1, i, keys_ref, value_ref, toward_end)
    copies[3].wait()
    copies[4].wait()


def second_kernel(core_ref, keys_ref, value_ref, across_ref, tab_ref, keep_ref):
    core = core_ref[0]
    across = across_ref[...]
    down = across.T
    last = down[GROUP - 1 :, :]
    blank = jnp.zeros((GROUP, 128 - 48), F32)
    tab_ref[...] = jnp.concatenate([down, jnp.exp(down), jnp.exp(last - down), blank], axis=1)
    toward_end = toward_last(across)
    for i in range(HALF):
        keep_ref[i * DH : (i + 1) * DH, :] = state_term(core, 0, i, keys_ref, value_ref, toward_end)


def merge_forward(core_ref, own_ref, other_ref, across_ref, out_ref, dec_ref):
    zero = core_ref[0] == 0
    mine = jnp.broadcast_to(across_ref[:HALF, GROUP - 1 :], (HALF, DH))
    theirs = other_ref[WIDE + HALF :, :]
    decay = mine + theirs
    factor = jnp.exp(jnp.where(zero, theirs, mine))
    dec_ref[:HALF, :] = jnp.exp(jnp.where(zero, mine, theirs))
    dec_ref[HALF:, :] = factor
    own_factor, other_factor = jnp.where(zero, factor, 1.0), jnp.where(zero, 1.0, factor)
    for i in range(HALF):
        at = slice(i * DH, (i + 1) * DH)
        out_ref[i, :DH, :] = own_factor[i : i + 1] * own_ref[at, :] + other_factor[i : i + 1] * other_ref[at, :]
        out_ref[i, DH:, :] = jnp.broadcast_to(decay[i : i + 1], (8, DH))


def merge_backward(core_ref, own_ref, other_ref, dec_ref, out_ref):
    zero = core_ref[0] == 0
    for i in range(HALF):
        own = own_ref[i * DH : (i + 1) * DH, :]
        other = other_ref[i * DH : (i + 1) * DH, :]
        a, b = jnp.where(zero, own, other), jnp.where(zero, other, own)
        out_ref[i] = a + dec_ref[i : i + 1, :] * b


def total_kernel(reverse, parts_ref, decays_ref, out_ref):
    order = list(range(8))[:: -1 if reverse else 1]
    total = parts_ref[order[0], :DH, :]
    for at in order[1:]:
        total = jnp.exp(decays_ref[at, DH : DH + 1, :]) * total + parts_ref[at, :DH, :]
    out_ref[:DH, :] = total
    decay = decays_ref[0, DH:, :]
    for at in range(1, 8):
        decay = decay + decays_ref[at, DH:, :]
    out_ref[DH:, :] = decay


def pair_kernel(reverse, place_ref, own_ref, near_ref, out_ref):
    place = 3 - place_ref[0] if reverse else place_ref[0]
    even = (place == 0) | (place == 2)
    own, near = own_ref[...], near_ref[...]
    first, second = jnp.where(even, own, near), jnp.where(even, near, own)
    out_ref[...] = jnp.exp(second[DH : DH + 1, :]) * first[:DH, :] + second[:DH, :]


def enter_kernel(reverse, place_ref, parts_ref, decays_ref, near_ref, far_ref, out_ref):
    place = 3 - place_ref[0] if reverse else place_ref[0]
    near = jnp.where((place == 1) | (place == 3), near_ref[...], 0.0)
    state = jnp.where(place >= 2, far_ref[...], 0.0)
    state = jnp.exp(near[DH : DH + 1, :]) * state + near[:DH, :]
    order = list(range(8))[:: -1 if reverse else 1]
    for at in order:
        out_ref[at] = state
        if at != order[-1]:
            state = jnp.exp(decays_ref[at, DH : DH + 1, :]) * state + parts_ref[at, :DH, :]


def leave_kernel(reverse, core_ref, enter_ref, own_ref, other_ref, dec_ref, keep_ref, send_ref):
    first = core_ref[0] == (1 if reverse else 0)
    base = HALF if reverse else 0
    for i in range(HALF):
        own = own_ref[i * DH : (i + 1) * DH, :]
        other = other_ref[i * DH : (i + 1) * DH, :]
        nearer = jnp.where(first, own, other)
        x = enter_ref[i]
        y = dec_ref[base + i : base + i + 1, :] * x + nearer
        keep_ref[i] = jnp.where(first, x, y)
        send_ref[i] = jnp.where(first, y, x)


LOW, HIGH = slice(0, DH), slice(DH, GROUP)


def causal(first, middle, last, upper=False):
    blank = jnp.zeros_like(first)
    top, bottom = ([first, middle], [blank, last]) if upper else ([first, blank], [middle, last])
    return jnp.concatenate([jnp.concatenate(top, axis=1), jnp.concatenate(bottom, axis=1)], axis=0)


def masked(array, weights, upper=False):
    middle = array[LOW, HIGH] if upper else array[HIGH, LOW]
    parts = (array[LOW, LOW], middle, array[HIGH, HIGH])
    return causal(*((part * weights[at]).astype(BF16) for at, part in enumerate(parts)), upper=upper)


def intra_kernel(
    role, core_ref, query_hbm, gate_hbm, mixed_hbm, keys_ref, value_ref, gain_ref, tab_ref, across_ref,
    intra_ref, normed_ref, turned_ref, weights_ref, weighted_ref, query_ref, gate_ref, mixed_ref, sems,
):
    core = core_ref[0]
    tab = tab_ref[...]
    half = pl.ds(pl.multiple_of((core if role == 0 else 1 - core) * WIDE, WIDE), WIDE)
    copies = [
        pltpu.make_async_copy(source.at[:, half], target, sems.at[at])
        for at, (source, target) in enumerate(
            ((query_hbm, query_ref), (gate_hbm, gate_ref), (mixed_hbm, mixed_ref))
        )
    ]
    for copy in copies:
        copy.start()
    rows = lax.broadcasted_iota(jnp.int32, (DH, DH), 0)
    cols = lax.broadcasted_iota(jnp.int32, (DH, DH), 1)
    lower, upper = rows >= cols, rows <= cols
    copies[0].wait()
    for i in range(HALF):
        at = columns(role, core, i)
        to = slice(i * DH, (i + 1) * DH)
        query, keys = query_ref[:, to], keys_ref[:, at]
        down = lanes(tab, 0, role, i)
        across = across_ref[role * HALF + i : role * HALF + i + 1, :]
        weights = (
            jnp.exp(jnp.where(lower, down[LOW] - across[:, LOW], -jnp.inf)),
            jnp.exp(down[HIGH] - across[:, LOW]),
            jnp.exp(jnp.where(lower, down[HIGH] - across[:, HIGH], -jnp.inf)),
            jnp.exp(jnp.where(upper, across[:, LOW] - down[LOW], -jnp.inf)),
            jnp.exp(across[:, HIGH] - down[LOW]),
            jnp.exp(jnp.where(upper, across[:, HIGH] - down[HIGH], -jnp.inf)),
        )
        for part, array in enumerate(weights):
            weights_ref[i, part] = array
        weighted_ref[i] = (turned(query) * jnp.exp(across)).astype(BF16)
        probs = masked(dot(query, keys, 1, 1), weights[:3])
        turned_ref[i] = masked(dot(keys, query, 1, 1), weights[3:], upper=True)
        intra_ref[:, to] = dot(probs, value_ref[:, at], 1, 0)
    copies[1].wait()
    copies[2].wait()
    for i in range(HALF):
        at = columns(role, core, i)
        to = slice(i * DH, (i + 1) * DH)
        opening = jax.nn.sigmoid(gate_ref[:, to].astype(F32))
        normed_ref[:, to] = mixed_ref[:, to].astype(F32) * opening * gain_ref[:, at]


def attend_kernel(role, core_ref, query_ref, state_ref, intra_ref, normed_ref, tab_ref, *refs):
    if role == 0:
        out_ref, squares_ref, products_ref = refs
        squares, products = jnp.zeros((GROUP, DH), F32), jnp.zeros((GROUP, DH), F32)
    else:
        squares_in, products_in, out_ref, sums_ref = refs
        squares, products = squares_in[...], products_in[...]
    core = core_ref[0]
    tab = tab_ref[...]
    for i in range(HALF):
        at = columns(role, core, i)
        to = slice(i * DH, (i + 1) * DH)
        inter = dot(query_ref[:, at], state_ref[i].astype(BF16), 1, 0)
        attention = intra_ref[:, to] + inter * lanes(tab, 1, role, i)
        out_ref[:, to] = attention
        squares = squares + attention * attention
        products = products + normed_ref[:, to] * attention
    if role == 0:
        squares_ref[...] = squares
        products_ref[...] = products
    else:
        both = [jnp.sum(array.T, axis=0, keepdims=True) for array in (squares, products)]
        sums_ref[...] = jnp.concatenate(both + [jnp.zeros((6, GROUP), F32)], axis=0)


def norm_terms(sums, terms_ref):
    scale = lax.rsqrt(sums[0:1, :] / FEATURES + EPSILON)
    projection = scale * sums[1:2, :] / FEATURES
    both = jnp.concatenate([scale, scale * projection, jnp.zeros((6, GROUP), F32)], axis=0)
    terms_ref[...] = jnp.concatenate([both.T, jnp.zeros((GROUP, DH - 8), F32)], axis=1)


def grad_kernel(attention_ref, normed_ref, weighted_ref, terms_ref, grad_ref, term_ref):
    scale, shift = terms_ref[:, 0:1], terms_ref[:, 1:2]
    for i in range(HALF):
        to = slice(i * DH, (i + 1) * DH)
        grad = (scale * (normed_ref[:, to] - attention_ref[:, to] * shift)).astype(BF16)
        grad_ref[:, to] = grad
        term_ref[i * DH : (i + 1) * DH, :] = dot(weighted_ref[i], grad, 1, 0)


def grad_first(
    attention_ref, normed_ref, weighted_ref, sum_a, sum_b, sum_c, sum_d, grad_ref, term_ref, terms_ref
):
    norm_terms((sum_a[...] + sum_b[...]) + (sum_c[...] + sum_d[...]), terms_ref)
    grad_kernel(attention_ref, normed_ref, weighted_ref, terms_ref, grad_ref, term_ref)


class Sender:
    def __init__(self, role, core, sems):
        self.side = core if role == 0 else 1 - core
        self.sems = sems
        self.copies = []

    def send(self, buf, out, start, width):
        away = pl.ds(pl.multiple_of(self.side * WIDE + start, width), width)
        copy = pltpu.make_async_copy(
            buf.at[:, start : start + width], out.at[:, away], self.sems.at[len(self.copies)]
        )
        copy.start()
        self.copies.append(copy)

    def wait(self):
        for copy in self.copies:
            copy.wait()


def inner_part(
    role, core, query_ref, keys_ref, value_ref, state_ref, grad_ref, turned_ref, weights_ref, tab, keys_out, value_out,
    query_buf, sender, query_out,
):
    for i in range(HALF):
        at = columns(role, core, i)
        to = slice(i * DH, (i + 1) * DH)
        query, keys, value, grad = query_ref[:, at], keys_ref[:, at], value_ref[:, at], grad_ref[:, to]
        weights = [weights_ref[i, part] for part in range(6)]
        scores = masked(dot(grad, value, 1, 1), weights[:3])
        flipped_scores = masked(dot(value, grad, 1, 1), weights[3:], upper=True)
        grad_query = dot(scores, keys, 1, 0)
        grad_query = grad_query + dot(grad, state_ref[i].astype(BF16), 1, 1) * lanes(tab, 1, role, i)
        query_buf[:, to] = grad_query.astype(BF16)
        keys_out[:, to] = dot(flipped_scores, query, 1, 0)
        value_out[:, to] = dot(turned_ref[i], grad, 1, 0)
        if i % 2 == 1:
            sender.send(query_buf, query_out, (i - 1) * DH, 2 * DH)


def local_kernel(
    role, core_ref, query_ref, keys_ref, value_ref, state_ref, grad_ref, turned_ref, weights_ref, tab_ref, mixed_ref,
    gate_ref, terms_ref, *refs
):
    query_out, mixed_out, gate_out, keys_out, value_out, query_buf, mixed_buf, gate_buf, sems = refs[-9:]
    core = core_ref[0]
    tab = tab_ref[...]
    scale = terms_ref[:, 0:1]
    sender = Sender(role, core, sems)
    for i in range(HALF):
        to = slice(i * DH, (i + 1) * DH)
        into = slice(role * WIDE + i * DH, role * WIDE + (i + 1) * DH)
        mixed_buf[:, to] = (mixed_ref[:, into] * scale).astype(BF16)
        gate_buf[:, to] = (gate_ref[:, into] * scale).astype(BF16)
        if i % 4 == 3:
            sender.send(mixed_buf, mixed_out, (i - 3) * DH, 4 * DH)
            sender.send(gate_buf, gate_out, (i - 3) * DH, 4 * DH)
    inner_part(
        role, core, query_ref, keys_ref, value_ref, state_ref, grad_ref, turned_ref, weights_ref, tab, keys_out, value_out,
        query_buf, sender, query_out,
    )
    sender.wait()


def opened_kernel(
    core_ref, gate_ref, gain_ref, upstream_ref, own_ref, other_ref, own_normed, other_normed, mixed_ref, gate_out
):
    core = core_ref[0]
    for role, ref, normed_ref in ((0, own_ref, own_normed), (1, other_ref, other_normed)):
        for i in range(HALF):
            at = columns(role, core, i)
            to = slice(i * DH, (i + 1) * DH)
            into = slice(role * WIDE + i * DH, role * WIDE + (i + 1) * DH)
            opening = jax.nn.sigmoid(gate_ref[:, at].astype(F32))
            attention = ref[:, to]
            mixed_ref[:, into] = attention * (gain_ref[:, at] * opening)
            gate_out[:, into] = normed_ref[:, to] * (attention * (1.0 - opening))


def last_kernel(
    role, core_ref, keys_ref, value_ref, state_ref, part_keys, part_value, tab_ref, *refs
):
    keys_out, value_out, keys_buf, value_buf, sems = refs[-5:]
    core = core_ref[0]
    tab = tab_ref[...]
    sender = Sender(role, core, sems)
    for i in range(HALF):
        at = columns(role, core, i)
        to = slice(i * DH, (i + 1) * DH)
        state = state_ref[i].astype(BF16)
        toward_end = lanes(tab, 2, role, i)
        grad_keys = part_keys[:, to] + dot(value_ref[:, at], state, 1, 1) * toward_end
        grad_value = part_value[:, to] + dot(keys_ref[:, at], state, 1, 0) * toward_end
        keys_buf[:, to] = grad_keys.astype(BF16)
        value_buf[:, to] = grad_value.astype(BF16)
        if i % 2 == 1:
            for buf, out in ((keys_buf, keys_out), (value_buf, value_out)):
                sender.send(buf, out, (i - 1) * DH, 2 * DH)
    sender.wait()


def swap(array):
    return lax.ppermute(array, "core", [(0, 1), (1, 0)])


def flipped(array, axis, flip):
    return lax.ppermute(array, axis, [(i, i ^ flip) for i in range(4)])


def spread(array):
    return lax.all_to_all(array, PLANE, 0, 0, tiled=True)


def scan(core, place, own, other, across, dec, decays, reverse, beside):
    if reverse:
        totals = call(merge_backward, shape(HALF, DH, DH), core, own, other, dec, name="merge_b")
    else:
        totals, dec = call(
            merge_forward, (shape(HALF, DH + 8, DH), shape(2 * HALF, DH)), core, own, other, across, name="merge_f"
        )
    parts = spread(totals)
    decays = parts if decays is None else decays
    row = call(
        functools.partial(total_kernel, reverse), shape(DH + 8, DH), parts, decays, smem=0, name="row_total"
    )
    near, done = lax.optimization_barrier((flipped(row, "z1", 1), beside(row, 0, ())))
    pair = call(functools.partial(pair_kernel, reverse), shape(DH, DH), place, row, near, name="pair")
    far, done = lax.optimization_barrier((flipped(pair, "z1", 3), beside(pair, 1, done)))
    entering = call(
        functools.partial(enter_kernel, reverse), shape(8, DH, DH), place, parts, decays, near, far, name="enter"
    )
    entering = spread(entering)
    keep, send = call(
        functools.partial(leave_kernel, reverse),
        (shape(HALF, DH, DH), shape(HALF, DH, DH)),
        core, entering, own, other, dec, name="leave",
    )
    return keep, swap(send), dec, decays, done


def on_device(query, keys, value, gate, decay, gain, upstream):
    core, place = lax.optimization_barrier(
        [lax.axis_index(axis).astype(jnp.int32).reshape(1) for axis in ("core", "z1")]
    )
    gain = gain.reshape(1, -1)
    big = 2 * GROUP * GROUP * DH * HALF
    small = big // 2

    full = shape(GROUP, 2 * WIDE, dtype=BF16)
    across, send, keys, value = call(
        first_kernel,
        (shape(16, GROUP), shape(WIDE + 16, DH), full, full),
        core, *(pltpu.with_memory_space_constraint(a, pltpu.HBM) for a in (keys, value, decay.T)),
        flops=small, name="first",
        specs=[SMEM, HBM, HBM, HBM], scratch=[pltpu.VMEM((16, GROUP), F32), pltpu.SemaphoreType.DMA((5,))],
    )
    other = swap(send)
    tab, own = call(
        second_kernel, (shape(GROUP, 128), shape(WIDE, DH)), core, keys, value, across, flops=small, name="second"
    )

    wide = shape(GROUP, WIDE)
    half = pltpu.VMEM((GROUP, WIDE), BF16)
    probs_shape = shape(HALF, GROUP, GROUP, dtype=BF16)
    weights_shape = shape(HALF, 6, DH, DH)
    weighted_shape = shape(HALF, DH, GROUP, dtype=BF16)

    def intra_part(after, role, done):
        table, _ = lax.optimization_barrier((tab, after))
        far = [pltpu.with_memory_space_constraint(array, pltpu.HBM) for array in (query, gate, upstream)]
        results = call(
            functools.partial(intra_kernel, role), (wide, wide, probs_shape, weights_shape, weighted_shape),
            core, *far, keys, value, gain, table, across, flops=3 * big, name=f"intra{role}", limit=8,
            specs=[SMEM] + [HBM] * 3 + [VMEM] * 5, scratch=[half] * 3 + [pltpu.SemaphoreType.DMA((3,))],
        )
        return (*done, results)

    state_own, state_other, dec, decays, intra = scan(
        core, place, own, other, across, None, None, False, intra_part
    )

    narrow = shape(GROUP, DH)
    att_own, *partial = call(
        functools.partial(attend_kernel, 0), (wide, narrow, narrow),
        core, query, state_own, *intra[0][:2], tab, flops=small, name="attend0",
    )
    att_other, sums = call(
        functools.partial(attend_kernel, 1), (wide, shape(8, GROUP)),
        core, query, state_other, *intra[1][:2], tab, *partial, flops=small, name="attend1",
    )
    opened = call(
        opened_kernel, (shape(GROUP, 2 * WIDE), shape(GROUP, 2 * WIDE)),
        core, gate, gain, upstream, att_own, att_other, intra[0][1], intra[1][1], name="opened",
    )
    moved = [flipped(sums, "head", flip) for flip in (1, 2, 3)]
    moved, opened = lax.optimization_barrier((moved, opened))

    grads_shape = (shape(GROUP, WIDE, dtype=BF16), shape(WIDE, DH))
    grad_other, term_send, terms = call(
        grad_first, (*grads_shape, shape(GROUP, DH)),
        att_other, intra[1][1], intra[1][4], sums, *moved, flops=small, smem=0, name="grad1",
    )
    term_other = swap(term_send)
    grad_own, term_own = call(
        grad_kernel, grads_shape, att_own, intra[0][1], intra[0][4], terms, flops=small, smem=0, name="grad0",
    )


    whole = pltpu.HBM((GROUP, 2 * WIDE), BF16)

    def local(after, role, done):
        held, factors, _ = lax.optimization_barrier((query, terms, after))
        state, grad = ((state_own, grad_own), (state_other, grad_other))[role]
        sent = done[:3]
        results = call(
            functools.partial(local_kernel, role), (whole, whole, whole, wide, wide),
            core, held, keys, value, state, grad, *intra[role][2:4], tab, *opened, factors, *sent,
            flops=5 * big, name=f"local{role}", limit=10,
            specs=[SMEM] + [VMEM] * 11 + [HBM] * len(sent), outs=(HBM, HBM, HBM, VMEM, VMEM),
            scratch=[half] * 3 + [pltpu.SemaphoreType.DMA((8,))],
            aliases={12: 0, 13: 1, 14: 2} if sent else None,
        )
        return (*results[:3], *done[3:], *results[3:])

    after_own, after_other, _, _, (grad_query, mixed, grad_gate, *inner) = scan(
        core, place, term_own, term_other, across, dec, decays, True, local
    )
    ends = ()
    for role, state in ((0, after_own), (1, after_other)):
        ends = call(
            functools.partial(last_kernel, role), (full, full),
            core, keys, value, state, *inner[2 * role : 2 * role + 2], tab, *ends, flops=2 * small, name=f"last{role}",
            specs=[SMEM] + [VMEM] * 6 + [HBM] * len(ends), outs=(HBM, HBM),
            scratch=[half, half, pltpu.SemaphoreType.DMA((8,))], aliases={7: 0, 8: 1} if ends else None,
        )
    grad_keys, grad_value = ends
    return mixed, grad_query, grad_keys, grad_value, grad_gate


def solution(mesh):
    levels = Mesh(mesh.devices.reshape(4, 2, 4, 2, 4), ("z1", "z0", "y", "core", "head"))
    seq = ("z1", "z0", "y", "core")
    both = P(seq, "head")
    return jax.shard_map(
        on_device,
        mesh=levels,
        in_specs=(both, both, both, both, both, P("head"), both),
        out_specs=(both,) * 5,
        check_vma=False,
    )
```

```python
import functools
import math

import jax
import jax.numpy as jnp
from jax import lax
from jax.experimental import pallas as pl
from jax.experimental.pallas import tpu as pltpu
from jax.sharding import Mesh, PartitionSpec as P

DH = 128
GROUP = 256
HALF = 8
WIDE = HALF * DH
FEATURES = 64 * DH
EPSILON = 1e-06
F32 = jnp.float32
BF16 = jnp.bfloat16
PLANE = ("z0", "y")
VMEM = pl.BlockSpec(memory_space=pltpu.VMEM)
SMEM = pl.BlockSpec(memory_space=pltpu.SMEM)
HBM = pl.BlockSpec(memory_space=pltpu.HBM)


def call(kernel, out, *args, flops=0, smem=1, limit=6, name=None, specs=None, outs=None, scratch=(), aliases=None):
    moved = sum(a.size * a.dtype.itemsize for a in args)
    moved += sum(math.prod(o.shape) * 4 for o in jax.tree.leaves(out))
    return pl.pallas_call(
        kernel,
        out_shape=out,
        in_specs=specs or [SMEM] * smem + [VMEM] * (len(args) - smem),
        out_specs=outs or jax.tree.map(lambda _: VMEM, out),
        scratch_shapes=scratch,
        input_output_aliases=aliases or {},
        compiler_params=pltpu.CompilerParams(vmem_limit_bytes=limit << 20),
        cost_estimate=pl.CostEstimate(flops=flops, bytes_accessed=moved, transcendentals=0),
        name=name,
    )(*args)


def shape(*dims, dtype=F32):
    return jax.ShapeDtypeStruct(dims, dtype)


def dot(a, b, ca, cb, precision=None):
    return lax.dot_general(
        a, b, (((ca,), (cb,)), ((), ())), precision=precision, preferred_element_type=F32
    )


def turned(x):
    rows = lax.broadcasted_iota(jnp.int32, (DH, DH), 0)
    cols = lax.broadcasted_iota(jnp.int32, (DH, DH), 1)
    return dot((rows == cols).astype(BF16), x, 1, 1)


def columns(role, core, i):
    side = core if role == 0 else 1 - core
    return pl.ds(pl.multiple_of(side * WIDE + i * DH, DH), DH)


def pairs(role, core, i):
    side = core if role == 0 else 1 - core
    return pl.ds(pl.multiple_of(side * WIDE + i * DH, 2 * DH), 2 * DH)


def both_lanes(tab, which, role, i):
    parts = [jnp.broadcast_to(lanes(tab, which, role, at), (GROUP, DH)) for at in (i, i + 1)]
    return jnp.concatenate(parts, axis=1)


def diagonal(first, second):
    blank = jnp.zeros_like(first)
    return jnp.concatenate(
        [jnp.concatenate([first, blank], axis=1), jnp.concatenate([blank, second], axis=1)], axis=0
    )


def lanes(tab, which, role, i):
    at = which * 16 + role * HALF + i
    return tab[:, at : at + 1]


def tables(core, decays):
    rows = lax.broadcasted_iota(jnp.int32, (GROUP, GROUP), 0)
    cols = lax.broadcasted_iota(jnp.int32, (GROUP, GROUP), 1)
    tri = (rows >= cols).astype(BF16)
    high = decays.astype(BF16)
    rest = decays - high.astype(F32)
    middle = rest.astype(BF16)
    low = (rest - middle.astype(F32)).astype(BF16)
    across = dot(jnp.concatenate([high, middle, low], axis=0), tri, 1, 1)
    across = across[:16] + (across[16:32] + across[32:])
    return jnp.where(core == 0, across, jnp.concatenate([across[HALF:], across[:HALF]], axis=0))


def state_term(core, role, i, keys_ref, value_ref, toward_end):
    at = columns(role, core, i)
    row = toward_end[role * HALF + i : role * HALF + i + 1, :]
    keyed = (turned(keys_ref[:, at]) * row).astype(BF16)
    return dot(keyed, value_ref[:, at], 1, 0)


def toward_last(across):
    return jnp.exp(across[:, GROUP - 1 :] - across)


def first_kernel(
    core_ref, keys_hbm, value_hbm, decay_hbm, across_ref, send_ref, keys_ref, value_ref, decay_ref, sems
):
    core = core_ref[0]
    copies = [pltpu.make_async_copy(decay_hbm, decay_ref, sems.at[0])]
    for role in (1, 0):
        at = pl.ds(pl.multiple_of((core if role == 0 else 1 - core) * WIDE, WIDE), WIDE)
        for source, target in ((keys_hbm, keys_ref), (value_hbm, value_ref)):
            copies.append(pltpu.make_async_copy(source.at[:, at], target.at[:, at], sems.at[len(copies)]))
    for copy in copies:
        copy.start()
    copies[0].wait()
    across = tables(core, decay_ref[...])
    across_ref[...] = across
    send_ref[WIDE:, :] = jnp.broadcast_to(across[:, GROUP - 1 :], (16, DH))
    toward_end = toward_last(across)
    copies[1].wait()
    copies[2].wait()
    for i in range(HALF):
        send_ref[i * DH : (i + 1) * DH, :] = state_term(core, 1, i, keys_ref, value_ref, toward_end)
    copies[3].wait()
    copies[4].wait()


def second_kernel(core_ref, keys_ref, value_ref, across_ref, tab_ref, keep_ref):
    core = core_ref[0]
    across = across_ref[...]
    down = across.T
    last = down[GROUP - 1 :, :]
    blank = jnp.zeros((GROUP, 128 - 48), F32)
    tab_ref[...] = jnp.concatenate([down, jnp.exp(down), jnp.exp(last - down), blank], axis=1)
    toward_end = toward_last(across)
    for i in range(HALF):
        keep_ref[i * DH : (i + 1) * DH, :] = state_term(core, 0, i, keys_ref, value_ref, toward_end)


def merge_forward(core_ref, own_ref, other_ref, across_ref, out_ref, dec_ref):
    zero = core_ref[0] == 0
    mine = jnp.broadcast_to(across_ref[:HALF, GROUP - 1 :], (HALF, DH))
    theirs = other_ref[WIDE + HALF :, :]
    decay = mine + theirs
    factor = jnp.exp(jnp.where(zero, theirs, mine))
    dec_ref[:HALF, :] = jnp.exp(jnp.where(zero, mine, theirs))
    dec_ref[HALF:, :] = factor
    own_factor, other_factor = jnp.where(zero, factor, 1.0), jnp.where(zero, 1.0, factor)
    for i in range(HALF):
        at = slice(i * DH, (i + 1) * DH)
        out_ref[i, :DH, :] = own_factor[i : i + 1] * own_ref[at, :] + other_factor[i : i + 1] * other_ref[at, :]
        out_ref[i, DH:, :] = jnp.broadcast_to(decay[i : i + 1], (8, DH))


def merge_backward(core_ref, own_ref, other_ref, dec_ref, out_ref):
    zero = core_ref[0] == 0
    for i in range(HALF):
        own = own_ref[i * DH : (i + 1) * DH, :]
        other = other_ref[i * DH : (i + 1) * DH, :]
        a, b = jnp.where(zero, own, other), jnp.where(zero, other, own)
        out_ref[i] = a + dec_ref[i : i + 1, :] * b


def total_kernel(reverse, parts_ref, decays_ref, out_ref):
    order = list(range(8))[:: -1 if reverse else 1]
    total = parts_ref[order[0], :DH, :]
    for at in order[1:]:
        total = jnp.exp(decays_ref[at, DH : DH + 1, :]) * total + parts_ref[at, :DH, :]
    out_ref[:DH, :] = total
    decay = decays_ref[0, DH:, :]
    for at in range(1, 8):
        decay = decay + decays_ref[at, DH:, :]
    out_ref[DH:, :] = decay


def pair_kernel(reverse, place_ref, own_ref, near_ref, out_ref):
    place = 3 - place_ref[0] if reverse else place_ref[0]
    even = (place == 0) | (place == 2)
    own, near = own_ref[...], near_ref[...]
    first, second = jnp.where(even, own, near), jnp.where(even, near, own)
    out_ref[...] = jnp.exp(second[DH : DH + 1, :]) * first[:DH, :] + second[:DH, :]


def enter_kernel(reverse, place_ref, parts_ref, decays_ref, near_ref, far_ref, out_ref):
    place = 3 - place_ref[0] if reverse else place_ref[0]
    near = jnp.where((place == 1) | (place == 3), near_ref[...], 0.0)
    state = jnp.where(place >= 2, far_ref[...], 0.0)
    state = jnp.exp(near[DH : DH + 1, :]) * state + near[:DH, :]
    order = list(range(8))[:: -1 if reverse else 1]
    for at in order:
        out_ref[at] = state
        if at != order[-1]:
            state = jnp.exp(decays_ref[at, DH : DH + 1, :]) * state + parts_ref[at, :DH, :]


def leave_kernel(reverse, send, core_ref, enter_ref, own_ref, other_ref, dec_ref, out_ref):
    first = core_ref[0] == (1 if reverse else 0)
    straight = ~first if send else first
    base = HALF if reverse else 0
    for i in range(HALF):
        own = own_ref[i * DH : (i + 1) * DH, :]
        other = other_ref[i * DH : (i + 1) * DH, :]
        x = enter_ref[i]
        y = dec_ref[base + i : base + i + 1, :] * x + jnp.where(first, own, other)
        out_ref[i] = jnp.where(straight, x, y)


LOW, HIGH = slice(0, DH), slice(DH, GROUP)


def causal(first, middle, last, upper=False):
    blank = jnp.zeros_like(first)
    top, bottom = ([first, middle], [blank, last]) if upper else ([first, blank], [middle, last])
    return jnp.concatenate([jnp.concatenate(top, axis=1), jnp.concatenate(bottom, axis=1)], axis=0)


def masked(array, weights, upper=False):
    middle = array[LOW, HIGH] if upper else array[HIGH, LOW]
    parts = (array[LOW, LOW], middle, array[HIGH, HIGH])
    return causal(*((part * weights[at]).astype(BF16) for at, part in enumerate(parts)), upper=upper)


def intra_kernel(
    role, core_ref, query_ref, keys_ref, value_ref, gate_ref, gain_ref, mixed_ref, tab_ref, across_ref,
    intra_ref, normed_ref, turned_ref, weights_ref, weighted_ref,
):
    core = core_ref[0]
    tab = tab_ref[...]
    rows = lax.broadcasted_iota(jnp.int32, (DH, DH), 0)
    cols = lax.broadcasted_iota(jnp.int32, (DH, DH), 1)
    lower, upper = rows >= cols, rows <= cols
    for i in range(HALF):
        at = columns(role, core, i)
        to = slice(i * DH, (i + 1) * DH)
        query, keys = query_ref[:, at], keys_ref[:, at]
        down = lanes(tab, 0, role, i)
        across = across_ref[role * HALF + i : role * HALF + i + 1, :]
        weights = (
            jnp.exp(jnp.where(lower, down[LOW] - across[:, LOW], -jnp.inf)),
            jnp.exp(down[HIGH] - across[:, LOW]),
            jnp.exp(jnp.where(lower, down[HIGH] - across[:, HIGH], -jnp.inf)),
            jnp.exp(jnp.where(upper, across[:, LOW] - down[LOW], -jnp.inf)),
            jnp.exp(across[:, HIGH] - down[LOW]),
            jnp.exp(jnp.where(upper, across[:, HIGH] - down[HIGH], -jnp.inf)),
        )
        for part, array in enumerate(weights):
            weights_ref[i, part] = array
        weighted_ref[i] = (turned(query) * jnp.exp(across)).astype(BF16)
        probs = masked(dot(query, keys, 1, 1), weights[:3])
        turned_ref[i] = masked(dot(keys, query, 1, 1), weights[3:], upper=True)
        intra_ref[:, to] = dot(probs, value_ref[:, at], 1, 0)
        opening = jax.nn.sigmoid(gate_ref[:, at].astype(F32))
        normed_ref[:, to] = mixed_ref[:, at].astype(F32) * opening * gain_ref[:, at]


def attend_kernel(role, core_ref, query_ref, state_ref, intra_ref, normed_ref, tab_ref, *refs):
    if role == 0:
        out_ref, squares_ref, products_ref = refs
        squares, products = jnp.zeros((GROUP, DH), F32), jnp.zeros((GROUP, DH), F32)
    else:
        squares_in, products_in, out_ref, sums_ref = refs
        squares, products = squares_in[...], products_in[...]
    core = core_ref[0]
    tab = tab_ref[...]
    for i in range(HALF):
        at = columns(role, core, i)
        to = slice(i * DH, (i + 1) * DH)
        inter = dot(query_ref[:, at], state_ref[i].astype(BF16), 1, 0)
        attention = intra_ref[:, to] + inter * lanes(tab, 1, role, i)
        out_ref[:, to] = attention
        squares = squares + attention * attention
        products = products + normed_ref[:, to] * attention
    if role == 0:
        squares_ref[...] = squares
        products_ref[...] = products
    else:
        both = [jnp.sum(array.T, axis=0, keepdims=True) for array in (squares, products)]
        sums_ref[...] = jnp.concatenate(both + [jnp.zeros((6, GROUP), F32)], axis=0)


def norm_terms(sums, terms_ref):
    scale = lax.rsqrt(sums[0:1, :] / FEATURES + EPSILON)
    projection = scale * sums[1:2, :] / FEATURES
    both = jnp.concatenate([scale, scale * projection, jnp.zeros((6, GROUP), F32)], axis=0)
    terms_ref[...] = jnp.concatenate([both.T, jnp.zeros((GROUP, DH - 8), F32)], axis=1)


def grad_kernel(attention_ref, normed_ref, weighted_ref, terms_ref, grad_ref, term_ref):
    scale, shift = terms_ref[:, 0:1], terms_ref[:, 1:2]
    for i in range(HALF):
        to = slice(i * DH, (i + 1) * DH)
        grad = (scale * (normed_ref[:, to] - attention_ref[:, to] * shift)).astype(BF16)
        grad_ref[:, to] = grad
        term_ref[i * DH : (i + 1) * DH, :] = dot(weighted_ref[i], grad, 1, 0)


def grad_first(
    attention_ref, normed_ref, weighted_ref, sum_a, sum_b, sum_c, sum_d, grad_ref, term_ref, terms_ref
):
    norm_terms((sum_a[...] + sum_b[...]) + (sum_c[...] + sum_d[...]), terms_ref)
    grad_kernel(attention_ref, normed_ref, weighted_ref, terms_ref, grad_ref, term_ref)


class Sender:
    def __init__(self, role, core, sems):
        self.side = core if role == 0 else 1 - core
        self.sems = sems
        self.copies = []

    def send(self, buf, out, start, width):
        away = pl.ds(pl.multiple_of(self.side * WIDE + start, width), width)
        copy = pltpu.make_async_copy(
            buf.at[:, start : start + width], out.at[:, away], self.sems.at[len(self.copies)]
        )
        copy.start()
        self.copies.append(copy)

    def wait(self):
        for copy in self.copies:
            copy.wait()


def inner_part(
    role, core, query_ref, keys_ref, value_ref, state_ref, grad_ref, turned_ref, weights_ref, tab, keys_out, value_out,
    query_buf, sender, query_out,
):
    for i in range(HALF):
        at = columns(role, core, i)
        to = slice(i * DH, (i + 1) * DH)
        query, keys, value, grad = query_ref[:, at], keys_ref[:, at], value_ref[:, at], grad_ref[:, to]
        weights = [weights_ref[i, part] for part in range(6)]
        scores = masked(dot(grad, value, 1, 1), weights[:3])
        flipped_scores = masked(dot(value, grad, 1, 1), weights[3:], upper=True)
        grad_query = dot(scores, keys, 1, 0)
        grad_query = grad_query + dot(grad, state_ref[i].astype(BF16), 1, 1) * lanes(tab, 1, role, i)
        query_buf[:, to] = grad_query.astype(BF16)
        keys_out[:, to] = dot(flipped_scores, query, 1, 0)
        value_out[:, to] = dot(turned_ref[i], grad, 1, 0)
        if i % 2 == 1:
            sender.send(query_buf, query_out, (i - 1) * DH, 2 * DH)


def local_kernel(
    role, core_ref, query_ref, keys_ref, value_ref, state_ref, grad_ref, turned_ref, weights_ref, tab_ref, mixed_ref,
    gate_ref, terms_ref, *refs
):
    query_out, mixed_out, gate_out, keys_out, value_out, query_buf, mixed_buf, gate_buf, sems = refs[-9:]
    core = core_ref[0]
    tab = tab_ref[...]
    scale = terms_ref[:, 0:1]
    sender = Sender(role, core, sems)
    for i in range(HALF):
        to = slice(i * DH, (i + 1) * DH)
        into = slice(role * WIDE + i * DH, role * WIDE + (i + 1) * DH)
        mixed_buf[:, to] = (mixed_ref[:, into] * scale).astype(BF16)
        gate_buf[:, to] = (gate_ref[:, into] * scale).astype(BF16)
        if i % 4 == 3:
            sender.send(mixed_buf, mixed_out, (i - 3) * DH, 4 * DH)
            sender.send(gate_buf, gate_out, (i - 3) * DH, 4 * DH)
    inner_part(
        role, core, query_ref, keys_ref, value_ref, state_ref, grad_ref, turned_ref, weights_ref, tab, keys_out, value_out,
        query_buf, sender, query_out,
    )
    sender.wait()


def opened_kernel(
    core_ref, gate_ref, gain_ref, upstream_ref, own_ref, other_ref, own_normed, other_normed, mixed_ref, gate_out
):
    core = core_ref[0]
    for role, ref, normed_ref in ((0, own_ref, own_normed), (1, other_ref, other_normed)):
        for i in range(HALF):
            at = columns(role, core, i)
            to = slice(i * DH, (i + 1) * DH)
            into = slice(role * WIDE + i * DH, role * WIDE + (i + 1) * DH)
            opening = jax.nn.sigmoid(gate_ref[:, at].astype(F32))
            attention = ref[:, to]
            mixed_ref[:, into] = attention * (gain_ref[:, at] * opening)
            gate_out[:, into] = normed_ref[:, to] * (attention * (1.0 - opening))


def last_kernel(
    role, core_ref, keys_ref, value_ref, state_ref, part_keys, part_value, tab_ref, *refs
):
    keys_out, value_out, keys_buf, value_buf, sems = refs[-5:]
    core = core_ref[0]
    tab = tab_ref[...]
    sender = Sender(role, core, sems)
    for i in range(0, HALF, 2):
        at = pairs(role, core, i)
        to = slice(i * DH, (i + 2) * DH)
        states = diagonal(state_ref[i].astype(BF16), state_ref[i + 1].astype(BF16))
        toward_end = both_lanes(tab, 2, role, i)
        grad_keys = part_keys[:, to] + dot(value_ref[:, at], states, 1, 1) * toward_end
        keys_buf[:, to] = grad_keys.astype(BF16)
        sender.send(keys_buf, keys_out, i * DH, 2 * DH)
        grad_value = part_value[:, to] + dot(keys_ref[:, at], states, 1, 0) * toward_end
        value_buf[:, to] = grad_value.astype(BF16)
        sender.send(value_buf, value_out, i * DH, 2 * DH)
    sender.wait()


def swap(array):
    return lax.ppermute(array, "core", [(0, 1), (1, 0)])


def flipped(array, axis, flip):
    return lax.ppermute(array, axis, [(i, i ^ flip) for i in range(4)])


def spread(array):
    return lax.all_to_all(array, PLANE, 0, 0, tiled=True)


def scan(core, place, own, other, across, dec, decays, reverse, beside):
    if reverse:
        totals = call(merge_backward, shape(HALF, DH, DH), core, own, other, dec, name="merge_b")
    else:
        totals, dec = call(
            merge_forward, (shape(HALF, DH + 8, DH), shape(2 * HALF, DH)), core, own, other, across, name="merge_f"
        )
    parts = spread(totals)
    decays = parts if decays is None else decays
    row = call(
        functools.partial(total_kernel, reverse), shape(DH + 8, DH), parts, decays, smem=0, name="row_total"
    )
    near, done = lax.optimization_barrier((flipped(row, "z1", 1), beside(row, 0, ())))
    pair = call(functools.partial(pair_kernel, reverse), shape(DH, DH), place, row, near, name="pair")
    far, done = lax.optimization_barrier((flipped(pair, "z1", 3), beside(pair, 1, done)))
    entering = call(
        functools.partial(enter_kernel, reverse), shape(8, DH, DH), place, parts, decays, near, far, name="enter"
    )
    entering = spread(entering)
    send, keep = (
        call(
            functools.partial(leave_kernel, reverse, away), shape(HALF, DH, DH), core, entering, own, other, dec,
            name="leave" if away else "keep",
        )
        for away in (True, False)
    )
    return keep, swap(send), dec, decays, done


def on_device(query, keys, value, gate, decay, gain, upstream):
    core, place = lax.optimization_barrier(
        [lax.axis_index(axis).astype(jnp.int32).reshape(1) for axis in ("core", "z1")]
    )
    gain = gain.reshape(1, -1)
    big = 2 * GROUP * GROUP * DH * HALF
    small = big // 2

    full = shape(GROUP, 2 * WIDE, dtype=BF16)
    across, send, keys, value = call(
        first_kernel,
        (shape(16, GROUP), shape(WIDE + 16, DH), full, full),
        core, *(pltpu.with_memory_space_constraint(a, pltpu.HBM) for a in (keys, value, decay.T)),
        flops=small, name="first",
        specs=[SMEM, HBM, HBM, HBM], scratch=[pltpu.VMEM((16, GROUP), F32), pltpu.SemaphoreType.DMA((5,))],
    )
    other = swap(send)
    tab, own = call(
        second_kernel, (shape(GROUP, 128), shape(WIDE, DH)), core, keys, value, across, flops=small, name="second"
    )

    wide = shape(GROUP, WIDE)
    probs_shape = shape(HALF, GROUP, GROUP, dtype=BF16)
    weights_shape = shape(HALF, 6, DH, DH)
    weighted_shape = shape(HALF, DH, GROUP, dtype=BF16)

    def intra_part(after, role, done):
        held, _ = lax.optimization_barrier((query, after))
        results = call(
            functools.partial(intra_kernel, role), (wide, wide, probs_shape, weights_shape, weighted_shape),
            core, held, keys, value, gate, gain, upstream, tab, across, flops=3 * big, name=f"intra{role}",
        )
        return (*done, results)

    state_own, state_other, dec, decays, intra = scan(
        core, place, own, other, across, None, None, False, intra_part
    )

    narrow = shape(GROUP, DH)
    att_own, *partial = call(
        functools.partial(attend_kernel, 0), (wide, narrow, narrow),
        core, query, state_own, *intra[0][:2], tab, flops=small, name="attend0",
    )
    att_other, sums = call(
        functools.partial(attend_kernel, 1), (wide, shape(8, GROUP)),
        core, query, state_other, *intra[1][:2], tab, *partial, flops=small, name="attend1",
    )
    opened = call(
        opened_kernel, (shape(GROUP, 2 * WIDE), shape(GROUP, 2 * WIDE)),
        core, gate, gain, upstream, att_own, att_other, intra[0][1], intra[1][1], name="opened",
    )
    moved = [flipped(sums, "head", flip) for flip in (1, 2, 3)]
    moved, opened = lax.optimization_barrier((moved, opened))

    grads_shape = (shape(GROUP, WIDE, dtype=BF16), shape(WIDE, DH))
    grad_other, term_send, terms = call(
        grad_first, (*grads_shape, shape(GROUP, DH)),
        att_other, intra[1][1], intra[1][4], sums, *moved, flops=small, smem=0, name="grad1",
    )
    term_other = swap(term_send)
    grad_own, term_own = call(
        grad_kernel, grads_shape, att_own, intra[0][1], intra[0][4], terms, flops=small, smem=0, name="grad0",
    )

    half = pltpu.VMEM((GROUP, WIDE), BF16)

    whole = pltpu.HBM((GROUP, 2 * WIDE), BF16)

    def local(after, role, done):
        held, factors, _ = lax.optimization_barrier((query, terms, after))
        state, grad = ((state_own, grad_own), (state_other, grad_other))[role]
        sent = done[:3]
        results = call(
            functools.partial(local_kernel, role), (whole, whole, whole, wide, wide),
            core, held, keys, value, state, grad, *intra[role][2:4], tab, *opened, factors, *sent,
            flops=5 * big, name=f"local{role}", limit=10,
            specs=[SMEM] + [VMEM] * 11 + [HBM] * len(sent), outs=(HBM, HBM, HBM, VMEM, VMEM),
            scratch=[half] * 3 + [pltpu.SemaphoreType.DMA((8,))],
            aliases={12: 0, 13: 1, 14: 2} if sent else None,
        )
        return (*results[:3], *done[3:], *results[3:])

    after_own, after_other, _, _, (grad_query, mixed, grad_gate, *inner) = scan(
        core, place, term_own, term_other, across, dec, decays, True, local
    )
    ends = ()
    for role, state in ((0, after_own), (1, after_other)):
        ends = call(
            functools.partial(last_kernel, role), (full, full),
            core, keys, value, state, *inner[2 * role : 2 * role + 2], tab, *ends, flops=2 * small, name=f"last{role}",
            specs=[SMEM] + [VMEM] * 6 + [HBM] * len(ends), outs=(HBM, HBM),
            scratch=[half, half, pltpu.SemaphoreType.DMA((8,))], aliases={7: 0, 8: 1} if ends else None,
        )
    grad_keys, grad_value = ends
    return mixed, grad_query, grad_keys, grad_value, grad_gate


def solution(mesh):
    levels = Mesh(mesh.devices.reshape(4, 2, 4, 2, 4), ("z1", "z0", "y", "core", "head"))
    seq = ("z1", "z0", "y", "core")
    both = P(seq, "head")
    return jax.shard_map(
        on_device,
        mesh=levels,
        in_specs=(both, both, both, both, both, P("head"), both),
        out_specs=(both,) * 5,
        check_vma=False,
    )
```
